512 devices in a mesh: ctx: 64 (over z, x_hi, core), tp: 8 (over y, x_lo).
Axes of the slice: x: 4 (x_hi: 2, x_lo: 2; x = x_hi * 2 + x_lo), y: 4, z: 16, core: 2. Of those that a mesh axis runs over, the one named last changes fastest.
Arguments:
- pre_q: bfloat16 [8192, 8192], P('ctx', 'tp'), may hold values from -90 to 90
- pre_k: bfloat16 [8192, 1024], P('ctx', 'tp'), may hold values from -4.5 to 4.5
- pre_v: bfloat16 [8192, 1024], P('ctx', 'tp'), may hold values from -6 to 6
- page_table: int32 [64, 96], P('ctx'), may hold values from 0 to 511, as said below
- dec_q: bfloat16 [256, 4, 8192], P('ctx', None, 'tp'), may hold values from -90 to 90
- dec_new_k: bfloat16 [256, 4, 1024], P('ctx', None, 'tp'), may hold values from -4.5 to 4.5
- dec_new_v: bfloat16 [256, 4, 1024], P('ctx', None, 'tp'), may hold values from -6 to 6
- cache_k: bfloat16 [256, 512, 1024], P('ctx', None, 'tp'), may hold values from -6 to 6
- cache_v: bfloat16 [256, 512, 1024], P('ctx', None, 'tp'), may hold values from -6 to 6
- cache_len: int32 [256], P('ctx'), may hold values from 1 to 512
- out_weight: bfloat16 [8192, 8192], P('tp', 'ctx'), may hold values from -3 to 3
Outputs:
- pre_out: bfloat16 [8192, 8192], P('ctx', 'tp')
- dec_out: bfloat16 [1024, 8192], P('tp', 'ctx')
The draws below stay inside these ranges and needn't reach their ends.
Inputs may be any that keep to these rules, and one draw needn't show every extreme that they name: `page_table`: each owner's row names at least one and at most 2 pages of every index of ctx (whose pages are 8 p to 8 p + 7 for index p), and no page twice.
All inputs are finite; a program needn't handle non-finite values.
Results may differ from the reference program's by a relative error of at most 0.019.
Values may be sent and summed in bfloat16 or wider, within the bound.
A program may use at most 64 MiB of HBM per device.

```python
import math
import jax
import jax.numpy as jnp
from jax import lax

D = 8192
QH = 64
KVH = 8
HD = 128
ROW_DEV = 4
CACHE = 512
PAGE = 16
STEPS = 4
PROMPT = 8192
ROWS = 256
P_DEV = 8
SLOTS = 96
N_CTX = 64


def prompt_keys(key):
    return jax.random.truncated_normal(key, -4.5, 4.5, (PROMPT, KVH * HD), jnp.float32)


def decode_keys(key):
    return jax.random.truncated_normal(key, -4.5, 4.5, (ROWS, STEPS, KVH * HD), jnp.float32)


def draw_pre_k(key, part):
    base_keys = prompt_keys(key)
    return base_keys.astype(jnp.bfloat16)


def draw_pre_q(key, part):
    key = jax.random.fold_in(key, 5)
    queries = jax.random.truncated_normal(key, -6.0, 6.0, (PROMPT, QH * HD), jnp.float32)
    return queries.astype(jnp.bfloat16)


def draw_dec_new_k(key, part):
    base_keys = decode_keys(key)
    return base_keys.astype(jnp.bfloat16)


def draw_dec_q(key, part):
    key = jax.random.fold_in(key, 9)
    queries = jax.random.truncated_normal(key, -6.0, 6.0, (ROWS, STEPS, QH * HD), jnp.float32)
    return queries.astype(jnp.bfloat16)


def draw_cache_len(key, part):
    key = jax.random.fold_in(key, 17)
    first_key, second_key = jax.random.split(key)
    lengths = jax.random.randint(first_key, (ROWS,), 1, CACHE + 1)
    full_row = jax.random.randint(second_key, (), 0, ROWS)
    return jnp.where(jnp.arange(ROWS) == full_row, CACHE, lengths).astype(jnp.int32)


def draw_page_table(key, part):
    key = jax.random.fold_in(key, 23)
    first_key, second_key, third_key = jax.random.split(key, 3)
    page_scores = jax.random.randint(first_key, (N_CTX, N_CTX, P_DEV), 0, 1 << 20) * P_DEV + jnp.arange(P_DEV)
    page_order = jnp.argsort(page_scores, axis=-1)
    first_page = page_order[:, :, 0]
    second_page = page_order[:, :, 1]
    source_scores = jax.random.randint(second_key, (N_CTX, N_CTX), 0, 1 << 20) * N_CTX + jnp.arange(N_CTX)
    extra_sources = jnp.argsort(source_scores, axis=-1)[:, :N_CTX // 2]
    base_slots = jnp.arange(N_CTX)[None, :] * P_DEV + first_page
    extra_slots = extra_sources * P_DEV + jnp.take_along_axis(second_page, extra_sources, axis=1)
    table = jnp.concatenate([base_slots, extra_slots], axis=1)
    slot_scores = jax.random.randint(third_key, (N_CTX, SLOTS), 0, 1 << 20) * SLOTS + jnp.arange(SLOTS)
    slot_order = jnp.argsort(slot_scores, axis=-1)
    return jnp.take_along_axis(table, slot_order, axis=1).astype(jnp.int32)


def shard_levels(key, dims, pieces, least, top_value):
    factor_of, own = 1.0, jax.random.fold_in(key, 6)
    for dim, blocks in pieces:
        steps = jnp.exp(jax.random.uniform(jax.random.fold_in(own, dim), (blocks,), jnp.float32, least / len(pieces), top_value / len(pieces)))
        factor_of = factor_of * jnp.repeat(steps, dims[dim] // blocks).reshape([-1 if axis == dim else 1 for axis in range(len(dims))])
    return factor_of


def centred(stream_key, extent, spread, most, cuts=(), kind=jnp.bfloat16):
    factor_of = shard_levels(stream_key, extent, cuts, -0.22, 0.18) if cuts else 1.0
    drawn = jax.random.normal(stream_key, extent, jnp.float32) * spread * factor_of
    return jnp.minimum(jnp.maximum(drawn, -most), most).astype(kind)


def setup_inputs(seed: int = 0) -> dict:
    keys = jax.random.split(jax.random.key(seed), 12)
    pre_q = draw_pre_q(jax.random.fold_in(keys[11], 71), 0)
    pre_k = draw_pre_k(jax.random.fold_in(keys[11], 71), 0)
    pre_v = centred(keys[2], (PROMPT, KVH * HD), 1.0, 6.0, ((0, 64), (1, 8)))
    page_table = draw_page_table(jax.random.fold_in(keys[11], 71), 0)
    dec_q = draw_dec_q(jax.random.fold_in(keys[11], 71), 0)
    dec_new_k = draw_dec_new_k(jax.random.fold_in(keys[11], 71), 0)
    dec_new_v = centred(keys[6], (ROWS, STEPS, KVH * HD), 1.0, 6.0, ((0, 64), (2, 8)))
    cache_k = centred(keys[7], (ROWS, CACHE, KVH * HD), 1.0, 6.0, ((0, 64), (2, 8)))
    cache_v = centred(keys[8], (ROWS, CACHE, KVH * HD), 1.0, 6.0, ((0, 64), (2, 8)))
    cache_len = draw_cache_len(jax.random.fold_in(keys[11], 71), 0)
    out_weight = centred(keys[10], (QH * HD, D), (max(1, QH * HD // (SLOTS * PAGE + CACHE))) ** -0.5, 3.0, ((0, 8), (1, 64)))
    return {"pre_q": pre_q, "pre_k": pre_k, "pre_v": pre_v, "page_table": page_table, "dec_q": dec_q, "dec_new_k": dec_new_k, "dec_new_v": dec_new_v, "cache_k": cache_k, "cache_v": cache_v, "cache_len": cache_len, "out_weight": out_weight}


NEGATIVE = -1e30


def keep_rounded(values):
    return lax.optimization_barrier(values.astype(jnp.bfloat16)).astype(jnp.float32)


def prompt_attention(pre_q, pre_k, pre_v):
    group_size = QH // KVH
    block_rows = math.gcd(PROMPT, 512)
    block_total = PROMPT // block_rows
    queries = pre_q.reshape(block_total, block_rows, KVH, group_size, HD).transpose(0, 2, 1, 3, 4)
    keys_all = pre_k.reshape(PROMPT, KVH, HD).transpose(1, 0, 2)
    values_all = pre_v.reshape(PROMPT, KVH, HD).transpose(1, 0, 2)
    key_pos = jnp.arange(PROMPT, dtype=jnp.int32)

    def one_block(items):
        query_block, block_start = items
        positions = block_start + jnp.arange(block_rows, dtype=jnp.int32)
        live_mask = (key_pos[None, :] <= positions[:, None])[None]

        def one_head(head_items):
            head_queries, head_keys, head_values = head_items
            scores = jnp.einsum("qgd,jd->gqj", head_queries.astype(jnp.float32), head_keys.astype(jnp.float32)) * HD ** -0.5
            scores = jnp.where(live_mask, scores, NEGATIVE)
            top_score = jnp.max(scores, axis=-1, keepdims=True)
            weights = jnp.where(live_mask, jnp.exp(scores - top_score), 0.0)
            totals = jnp.sum(weights, axis=-1)
            mixed = jnp.einsum("gqj,jd->gqd", keep_rounded(weights), head_values.astype(jnp.float32))
            return mixed / totals[..., None]

        heads_out = lax.map(one_head, (query_block, keys_all, values_all))
        return heads_out.transpose(2, 0, 1, 3).reshape(block_rows, QH * HD).astype(jnp.bfloat16)

    starts = jnp.arange(block_total, dtype=jnp.int32) * block_rows
    return lax.map(one_block, (queries, starts)).reshape(PROMPT, QH * HD)


def decode_attention(page_table, pre_k, pre_v, dec_q, dec_new_k, dec_new_v, cache_k, cache_v, cache_len):
    group_size = QH // KVH
    page_total = PROMPT // PAGE
    pool_keys = pre_k.reshape(page_total, PAGE, KVH * HD)[page_table].reshape(N_CTX, SLOTS * PAGE, KVH, HD)
    pool_values = pre_v.reshape(page_total, PAGE, KVH * HD)[page_table].reshape(N_CTX, SLOTS * PAGE, KVH, HD)
    owners = jnp.arange(ROWS, dtype=jnp.int32) // ROW_DEV
    step_ids = jnp.arange(STEPS, dtype=jnp.int32)
    new_mask = step_ids[None, :] <= step_ids[:, None]
    cache_ids = jnp.arange(CACHE, dtype=jnp.int32)

    def one_row(items):
        row_queries, new_keys, new_values, old_keys, old_values, length, owner = items
        keys_row = jnp.concatenate([pool_keys[owner], old_keys.reshape(CACHE, KVH, HD), new_keys.reshape(STEPS, KVH, HD)], axis=0)
        values_row = jnp.concatenate([pool_values[owner], old_values.reshape(CACHE, KVH, HD), new_values.reshape(STEPS, KVH, HD)], axis=0)
        live_mask = jnp.concatenate([
            jnp.ones((STEPS, SLOTS * PAGE), dtype=bool),
            jnp.broadcast_to(cache_ids[None, :] < length, (STEPS, CACHE)),
            new_mask], axis=1)[:, None, None, :]
        queries_row = row_queries.reshape(STEPS, KVH, group_size, HD).astype(jnp.float32)
        scores = jnp.einsum("tkgd,jkd->tkgj", queries_row, keys_row.astype(jnp.float32)) * HD ** -0.5
        scores = jnp.where(live_mask, scores, NEGATIVE)
        top_score = jnp.max(scores, axis=-1, keepdims=True)
        weights = jnp.where(live_mask, jnp.exp(scores - top_score), 0.0)
        totals = jnp.sum(weights, axis=-1)
        mixed = jnp.einsum("tkgj,jkd->tkgd", keep_rounded(weights), values_row.astype(jnp.float32)) / totals[..., None]
        return mixed.reshape(STEPS, QH * HD).astype(jnp.bfloat16)

    return lax.map(one_row, (dec_q, dec_new_k, dec_new_v, cache_k, cache_v, cache_len, owners))


def reference(pre_q, pre_k, pre_v, page_table, dec_q, dec_new_k, dec_new_v, cache_k, cache_v, cache_len, out_weight):
    pre_out = prompt_attention(pre_q, pre_k, pre_v)
    attention = decode_attention(page_table, pre_k, pre_v, dec_q, dec_new_k, dec_new_v, cache_k, cache_v, cache_len)
    attention = attention.reshape(ROWS * STEPS, QH * HD)
    dec_out = jnp.dot(attention, out_weight, preferred_element_type=jnp.float32).astype(jnp.bfloat16)
    return (pre_out, dec_out)
```

```python
import functools
import math

import jax
import jax.numpy as jnp
from jax import lax
from jax.experimental import pallas as pl
from jax.experimental.pallas import tpu as pltpu
from jax.sharding import PartitionSpec as P

MESH = pl.DeviceIdType.MESH
HD = 128
GROUP = 8
PAGE = 16
STEPS = 4
NEGATIVE = -1e30
SCALE = HD ** -0.5 * math.log2(math.e)
F32 = jnp.float32
BF16 = jnp.bfloat16


def dot_t(a, b):
    return lax.dot_general(a, b, (((1,), (1,)), ((), ())), preferred_element_type=F32)


def dot(a, b):
    return jnp.dot(a, b, preferred_element_type=F32)


def wide(a, n):
    return jnp.concatenate([a] * n, axis=1)


def with_ones(values):
    return jnp.concatenate([values, jnp.ones(values.shape, BF16)], axis=1)


def row_max(scores):
    top = jnp.max(scores, axis=1, keepdims=True)
    return jnp.broadcast_to(top, (scores.shape[0], HD))


def kernel(
    nz, ntp,
    q_hbm, k_hbm, v_hbm, table, dq_ref, nk_ref, nv_ref, ck_hbm, cv_hbm, lens, w_hbm,
    pre_hbm, dec_hbm,
    kv, qv, ck, cv, wv, acc, top, dq32, nk32, nv32, dacc, dtop, pool_k, pool_v,
    att, sbuf, rbuf, prev, decv,
    loc, zs, zr, ss, sr, os, orr, xs, xr, ws, wr, at_s, at_r, rs, rr,
):
    half = nz // 2
    plane = ntp * 4
    ctx = lax.axis_index("ctx")
    tp = lax.axis_index("tp")
    z, xh, c = ctx // 4, (ctx // 2) % 2, ctx % 2
    mine = ctx % 4
    slots = table.shape[1]

    def device(zz, xx, cc):
        return (zz * 4 + xx * 2 + cc, tp)

    def move(src, dst, send, recv, to):
        return pltpu.make_async_remote_copy(
            src_ref=src, dst_ref=dst, send_sem=send, recv_sem=recv, device_id=to, device_id_type=MESH
        )

    sibling = device(z, xh, 1 - c)
    beside = device(z, 1 - xh, c)
    across = device(z, 1 - xh, 1 - c)

    def toward(d):
        return device(lax.rem(z + (1 if d == 0 else nz - 1), nz), xh, c)

    def block(d, s):
        return lax.rem(jnp.where(d == 0, z + nz - s, z + s), nz)

    def side(p):
        return xh if p == 0 else 1 - xh

    loads = [
        pltpu.make_async_copy(k_hbm, kv.at[z, c, xh, 0], loc.at[0]),
        pltpu.make_async_copy(v_hbm, kv.at[z, c, xh, 1], loc.at[1]),
        pltpu.make_async_copy(w_hbm, wv.at[xh, c], loc.at[2]),
        pltpu.make_async_copy(q_hbm, qv, loc.at[3]),
        pltpu.make_async_copy(ck_hbm, ck, loc.at[4]),
        pltpu.make_async_copy(cv_hbm, cv, loc.at[5]),
    ]
    for load in loads:
        load.start()
    barrier = pltpu.get_barrier_semaphore()
    here = tp * 4 + mine

    def greet(o, _):
        to = lax.rem(here + o, plane)
        pl.semaphore_signal(barrier, inc=1, device_id=(z * 4 + to % 4, to // 4), device_id_type=MESH)
        return 0

    for d in (0, 1):
        pl.semaphore_signal(barrier, inc=1, device_id=toward(d), device_id_type=MESH)
    lax.fori_loop(1, plane, greet, 0)
    loads[0].wait()
    loads[1].wait()
    pl.semaphore_wait(barrier, plane + 1)

    def along(d, p, s, zb):
        ref = kv.at[zb, c, side(p)]
        return move(ref, ref, zs.at[d, p, s - 1], zr.at[d, p, s - 1], toward(d))

    def over(d, p, s, cc):
        ref = kv.at[block(d, s), cc, side(p)]
        return move(ref, ref, ss.at[d, p, s - 1], sr.at[d, p, s - 1], sibling)

    def over_own(p, cc):
        ref = kv.at[z, cc, side(p)]
        return move(ref, ref, os.at[p], orr.at[p], sibling)

    def swap(p):
        ref = kv.at[z, c, side(p)]
        return move(ref, ref, xs, xr, beside)

    peers = ((sibling, xh, 1 - c), (beside, 1 - xh, c), (across, 1 - xh, 1 - c))

    def weight(n, xx, cc):
        ref = wv.at[xx, cc]
        return move(ref, ref, ws.at[n], wr.at[n], peers[n][0])

    def sends(p, d):
        return half > 1 or p == d

    swap(0).start()
    for d in (0, 1):
        if sends(0, d):
            along(d, 0, 1, z).start()
    over_own(0, c).start()
    swap(1).wait_recv()
    for d in (0, 1):
        if sends(1, d):
            along(d, 1, 1, z).start()
    over_own(1, c).start()
    loads[2].wait()
    for n in range(3):
        weight(n, xh, c).start()
    for load in loads[3:]:
        load.wait()

    for r in range(4):
        dq32[pl.ds(r * STEPS, STEPS), :] = dq_ref[r].astype(F32)
    nk32[...] = jnp.zeros_like(nk32)
    nv32[...] = jnp.zeros_like(nv32)
    for r in range(4):
        nk32[pl.ds(r * STEPS, STEPS), :] = nk_ref[r].astype(F32)
        nv32[pl.ds(r * STEPS, STEPS), :] = nv_ref[r].astype(F32)

    def decode_queries():
        rows = dq32[...].astype(BF16)
        return jnp.concatenate([rows[:, h * HD:(h + 1) * HD] for h in range(GROUP)], axis=0)

    queries = decode_queries()
    rows = queries.shape[0]

    def own_decode():
        cache = ck.shape[1]
        q_id = lax.broadcasted_iota(jnp.int32, (rows, cache), 0)
        k_id = lax.broadcasted_iota(jnp.int32, (rows, cache), 1)
        q_row = (q_id >> 2) & 3
        scores = []
        for r in range(4):
            live = (q_row == r) & (k_id < lens[r])
            scores.append(jnp.where(live, dot_t(queries, ck[r]), NEGATIVE))
        n_id = lax.broadcasted_iota(jnp.int32, (rows, HD), 0)
        u_id = lax.broadcasted_iota(jnp.int32, (rows, HD), 1)
        live = ((u_id >> 2) == ((n_id >> 2) & 3)) & ((u_id & 3) <= (n_id & 3))
        scores.append(jnp.where(live, dot_t(queries, nk32[...].astype(BF16)), NEGATIVE))
        most = row_max(scores[-1])
        for r in range(4):
            most = jnp.maximum(most, row_max(scores[r]))
        total = jnp.zeros((rows, 2 * HD), F32)
        for r in range(4):
            weights = jnp.exp2((scores[r] - wide(most, cache // HD)) * SCALE)
            total += dot(weights.astype(BF16), with_ones(cv[r]))
        weights = jnp.exp2((scores[-1] - most) * SCALE)
        total += dot(weights.astype(BF16), with_ones(nv32[...].astype(BF16)))
        dacc[...] = total
        dtop[...] = most

    own_decode()

    order = ((0, 0), (0, 1), (1, 0), (1, 1))
    tokens = qv.shape[0]
    span = 4 * tokens

    def attend(zb, masked):
        keys = jnp.concatenate([kv[zb, cc, xx, 0].reshape(tokens, HD) for cc, xx in order], axis=0)
        values = with_ones(
            jnp.concatenate([kv[zb, cc, xx, 1].reshape(tokens, HD) for cc, xx in order], axis=0)
        )
        live = None
        if masked:
            q_id = lax.broadcasted_iota(jnp.int32, (2 * tokens, span), 0) & (tokens - 1)
            k_id = lax.broadcasted_iota(jnp.int32, (2 * tokens, span), 1)
            place = k_id // tokens
            place = (place & 1) * 2 + (place >> 1)
            live = place * tokens + (k_id & (tokens - 1)) <= mine * tokens + q_id
        for pair in range(GROUP // 2):
            first = 2 * pair * HD
            q2 = jnp.concatenate([qv[:, first:first + HD], qv[:, first + HD:first + 2 * HD]], axis=0)
            scores = dot_t(q2, keys)
            if masked:
                scores = jnp.where(live, scores, NEGATIVE)
                most = row_max(scores)
            else:
                old = top[pair]
                most = jnp.maximum(old, row_max(scores))
            weights = jnp.exp2((scores - wide(most, span // HD)) * SCALE)
            mixed = dot(weights.astype(BF16), values)
            if not masked:
                mixed += acc[pair] * wide(jnp.exp2((old - most) * SCALE), 2)
            acc[pair] = mixed
            top[pair] = most

    for p in (0, 1):
        over_own(p, 1 - c).wait_recv()
    attend(z, True)

    def attend_step(d, s):
        needed = jnp.where(d == 0, z - s >= 0, z + s >= nz)

        @pl.when(needed)
        def _():
            attend(block(d, s), False)

    def wait_over(s, pieces):
        for p, d in pieces:
            over(d, p, s, 1 - c).wait_recv()

    every = [(p, d) for p in (0, 1) for d in (0, 1)]
    last = [(0, 0), (1, 1)]

    def ring(s, _):
        for p, d in every:
            zb = block(d, s)
            along(d, p, s, zb).wait_recv()
            if p == d:
                along(d, p, s + 1, zb).start()
            else:
                @pl.when(s < half - 1)
                def _():
                    along(d, p, s + 1, zb).start()
            over(d, p, s, c).start()

        @pl.when(s > 1)
        def _():
            wait_over(s - 1, every)

            def both(d, _):
                attend_step(d, s - 1)
                return 0

            lax.fori_loop(0, 2, both, 0)

        return 0

    lax.fori_loop(1, half, ring, 0)
    for p, d in last:
        along(d, p, half, block(d, half)).wait_recv()
        over(d, p, half, c).start()
    if half > 1:
        wait_over(half - 1, every)
    wait_over(half, last)

    def fetch(slot, _):
        page = table[0, slot]
        zz, xx, cc, at = page >> 5, (page >> 4) & 1, (page >> 3) & 1, page & 7
        pool_k[slot] = kv[zz, cc, xx, 0, at]
        pool_v[slot] = kv[zz, cc, xx, 1, at]
        return 0

    lax.fori_loop(0, slots, fetch, 0, unroll=8)
    scores = dot_t(queries, pool_k[...].reshape(slots * PAGE, HD))
    most = jnp.maximum(dtop[...], row_max(scores))
    weights = jnp.exp2((scores - wide(most, slots * PAGE // HD)) * SCALE)
    total = dot(weights.astype(BF16), with_ones(pool_v[...].reshape(slots * PAGE, HD)))
    total += dacc[...] * wide(jnp.exp2((dtop[...] - most) * SCALE), 2)
    mixed = (total[:, :HD] / total[:, HD:]).astype(BF16)
    lines = rows // GROUP
    for h in range(GROUP):
        att[z, h // 4, h % 4] = mixed[h * lines:(h + 1) * lines]

    def share(d, s, zb):
        return move(att.at[zb], att.at[zb], at_s.at[d, s - 1], at_r.at[d, s - 1], toward(d))

    def share_half(d, zb):
        ref = att.at[zb, d]
        return move(ref, ref, at_s.at[d, half - 1], at_r.at[d, half - 1], toward(d))

    for d in (0, 1):
        if half > 1:
            share(d, 1, z).start()
        else:
            share_half(d, z).start()

    def pass_on(s, _):
        for d in (0, 1):
            zb = block(d, s)
            share(d, s, zb).wait_recv()

            @pl.when(s < half - 1)
            def _():
                share(d, s + 1, zb).start()

            @pl.when(s == half - 1)
            def _():
                share_half(d, zb).start()

        return 0

    lax.fori_loop(1, half, pass_on, 0)
    for n in range(3):
        weight(n, peers[n][1], peers[n][2]).wait_recv()
    for d in (0, 1):
        share_half(d, block(d, half)).wait_recv()

    lhs = jnp.concatenate(
        [att[:, h // 4, h % 4].reshape(nz * lines, HD) for h in range(GROUP)], axis=1
    )
    depth = sbuf.shape[2]
    for xx in (0, 1):
        part = dot(lhs, jnp.concatenate([wv[xx, 0], wv[xx, 1]], axis=1)).astype(BF16)
        for cc in (0, 1):
            for j in range(ntp):
                sbuf[j, xx * 2 + cc] = part[j * depth:(j + 1) * depth, cc * HD:(cc + 1) * HD]

    def deal(o, to, source):
        return move(
            sbuf.at[to // 4, to % 4],
            rbuf.at[source // 4, source % 4],
            rs.at[o - 1],
            rr.at[o - 1],
            (z * 4 + to % 4, to // 4),
        )

    def deal_out(o, _):
        deal(o, lax.rem(here + o, plane), here).start()
        return 0

    lax.fori_loop(1, plane, deal_out, 0)
    rbuf[tp, mine] = sbuf[tp, mine]

    def rest(n, _):
        attend_step(n % 2, half - 1 + n // 2)
        return 0

    lax.fori_loop(0 if half > 1 else 2, 3, rest, 0)
    for pair in range(GROUP // 2):
        total = acc[pair]
        out = (total[:, :HD] / total[:, HD:]).astype(BF16)
        for n in (0, 1):
            first = (2 * pair + n) * HD
            prev[:, first:first + HD] = out[n * tokens:(n + 1) * tokens]
    store_pre = pltpu.make_async_copy(prev, pre_hbm, loc.at[6])
    store_pre.start()

    def deal_in(o, _):
        deal(o, lax.rem(here + o, plane), lax.rem(here + plane - o, plane)).wait_recv()
        return 0

    lax.fori_loop(1, plane, deal_in, 0)
    for n in range(4):
        total = rbuf[0, n].astype(F32)
        for j in range(1, ntp):
            total += rbuf[j, n].astype(F32)
        total = total.astype(BF16)
        for zz in range(depth // lines):
            decv[zz * 4 + n] = total[zz * lines:(zz + 1) * lines]
    store_dec = pltpu.make_async_copy(decv, dec_hbm, loc.at[7])
    store_dec.start()

    def ring_sent(s, _):
        for p, d in every:
            along(d, p, s, block(d, s - 1)).wait_send()
            over(d, p, s, c).wait_send()
        return 0

    lax.fori_loop(1, half, ring_sent, 0)
    for p, d in last:
        along(d, p, half, block(d, half - 1)).wait_send()
        over(d, p, half, c).wait_send()
    swap(0).wait_send()
    for p in (0, 1):
        over_own(p, c).wait_send()
    for n in range(3):
        weight(n, xh, c).wait_send()
    for d in (0, 1):
        def shared(s, _):
            share(d, s, block(d, s - 1)).wait_send()
            return 0

        lax.fori_loop(1, half, shared, 0)
        share_half(d, block(d, half - 1)).wait_send()

    def dealt(o, _):
        deal(o, lax.rem(here + o, plane), here).wait_send()
        return 0

    lax.fori_loop(1, plane, dealt, 0)
    store_pre.wait()
    store_dec.wait()


def local(pre_q, pre_k, pre_v, page_table, dec_q, dec_new_k, dec_new_v, cache_k, cache_v, cache_len, out_weight):
    nz = lax.axis_size("ctx") // 4
    ntp = lax.axis_size("tp")
    half = nz // 2
    tokens = pre_q.shape[0]
    pages = tokens // PAGE
    row_dev, cache = cache_k.shape[:2]
    slots = page_table.shape[1]
    lines = row_dev * STEPS
    plane = 4 * ntp
    out_rows = nz * 4 * lines // ntp
    depth = nz // ntp * lines
    any_space = pl.BlockSpec(memory_space=pl.ANY)
    vmem = pl.BlockSpec(memory_space=pltpu.VMEM)
    smem = pl.BlockSpec(memory_space=pltpu.SMEM)
    sem = pltpu.SemaphoreType.DMA
    pre_out, dec_out = pl.pallas_call(
        functools.partial(kernel, nz, ntp),
        out_shape=(
            jax.ShapeDtypeStruct((tokens, GROUP * HD), BF16),
            jax.ShapeDtypeStruct((out_rows // lines, lines, HD), BF16),
        ),
        in_specs=[
            any_space, any_space, any_space, smem, vmem, vmem, vmem,
            any_space, any_space, smem, any_space,
        ],
        out_specs=(any_space, any_space),
        scratch_shapes=[
            pltpu.VMEM((nz, 2, 2, 2, pages, PAGE, HD), BF16),
            pltpu.VMEM((tokens, GROUP * HD), BF16),
            pltpu.VMEM((row_dev, cache, HD), BF16),
            pltpu.VMEM((row_dev, cache, HD), BF16),
            pltpu.VMEM((2, 2, GROUP * HD, HD), BF16),
            pltpu.VMEM((GROUP // 2, 2 * tokens, 2 * HD), F32),
            pltpu.VMEM((GROUP // 2, 2 * tokens, HD), F32),
            pltpu.VMEM((lines, GROUP * HD), F32),
            pltpu.VMEM((HD, HD), F32),
            pltpu.VMEM((HD, HD), F32),
            pltpu.VMEM((GROUP * lines, 2 * HD), F32),
            pltpu.VMEM((GROUP * lines, HD), F32),
            pltpu.VMEM((slots, PAGE, HD), BF16),
            pltpu.VMEM((slots, PAGE, HD), BF16),
            pltpu.VMEM((nz, 2, 4, lines, HD), BF16),
            pltpu.VMEM((ntp, 4, depth, HD), BF16),
            pltpu.VMEM((ntp, 4, depth, HD), BF16),
            pltpu.VMEM((tokens, GROUP * HD), BF16),
            pltpu.VMEM((out_rows // lines, lines, HD), BF16),
            sem((8,)),
            sem((2, 2, half)), sem((2, 2, half)),
            sem((2, 2, half)), sem((2, 2, half)),
            sem((2,)), sem((2,)),
            sem(()), sem(()),
            sem((3,)), sem((3,)),
            sem((2, half)), sem((2, half)),
            sem((plane - 1,)), sem((plane - 1,)),
        ],
        compiler_params=pltpu.CompilerParams(
            collective_id=0, has_side_effects=True, vmem_limit_bytes=40 << 20
        ),
    )(
        pre_q,
        pre_k.reshape(pages, PAGE, HD),
        pre_v.reshape(pages, PAGE, HD),
        page_table,
        dec_q,
        dec_new_k,
        dec_new_v,
        cache_k,
        cache_v,
        cache_len,
        out_weight,
    )
    return (pre_out, dec_out.reshape(out_rows, HD))


def solution(mesh):
    placed = (
        P("ctx", "tp"),
        P("ctx", "tp"),
        P("ctx", "tp"),
        P("ctx", None),
        P("ctx", None, "tp"),
        P("ctx", None, "tp"),
        P("ctx", None, "tp"),
        P("ctx", None, "tp"),
        P("ctx", None, "tp"),
        P("ctx"),
        P("tp", "ctx"),
    )
    return jax.shard_map(
        local,
        mesh=mesh,
        in_specs=placed,
        out_specs=(P("ctx", "tp"), P("tp", "ctx")),
        check_vma=False,
    )
```

```python
import functools
import math

import jax
import jax.numpy as jnp
from jax import lax
from jax.experimental import pallas as pl
from jax.experimental.pallas import tpu as pltpu
from jax.sharding import PartitionSpec as P

MESH = pl.DeviceIdType.MESH
HD = 128
GROUP = 8
STEPS = 4
NEGATIVE = -1e30
SCALE = HD ** -0.5 * math.log2(math.e)
F32 = jnp.float32
BF16 = jnp.bfloat16


def dot_t(a, b):
    return lax.dot_general(a, b, (((1,), (1,)), ((), ())), preferred_element_type=F32)


def dot(a, b):
    return jnp.dot(a, b, preferred_element_type=F32)


def wide(a, n):
    return jnp.concatenate([a] * n, axis=1)


def with_ones(values):
    return jnp.concatenate([values, jnp.ones(values.shape, BF16)], axis=1)


def row_max(scores):
    top = jnp.max(scores, axis=1, keepdims=True)
    return jnp.broadcast_to(top, (scores.shape[0], HD))


def kernel(
    nz, ntp,
    q_hbm, k_hbm, v_hbm, table_hbm, dq_hbm, nk_hbm, nv_hbm, ck_hbm, cv_hbm, lens_hbm, w_hbm,
    pre_hbm, dec_hbm,
    table, lens, dq_in, nk_in, nv_in,
    kv, qv, ck, cv, wv, acc, top, dq32, nk32, nv32, dqs, flags, bias, dacc, dtop,
    ob, ost, db, dst, att, sbuf, rbuf, prev, decv,
    loc, zs, zr, ss, sr, os, orr, xs, xr, ws, wr, at_s, at_r, rs, rr,
):
    half = nz // 2
    plane = ntp * 4
    ctx = lax.axis_index("ctx")
    tp = lax.axis_index("tp")
    z, xh, c = ctx // 4, (ctx // 2) % 2, ctx % 2
    mine = ctx % 4
    here = tp * 4 + mine
    tokens = qv.shape[1]
    cache = ck.shape[1]
    slots = table.shape[1]
    lines = dq32.shape[0]
    rows = GROUP * lines

    def device(zz, xx, cc):
        return (zz * 4 + xx * 2 + cc, tp)

    def move(src, dst, send, recv, to):
        return pltpu.make_async_remote_copy(
            src_ref=src, dst_ref=dst, send_sem=send, recv_sem=recv, device_id=to, device_id_type=MESH
        )

    sibling = device(z, xh, 1 - c)
    beside = device(z, 1 - xh, c)

    def toward(d):
        return device(lax.rem(z + (1 if d == 0 else nz - 1), nz), xh, c)

    def block(d, s):
        return lax.rem(jnp.where(d == 0, z + nz - s, z + s), nz)

    loads = [
        pltpu.make_async_copy(a, b, loc.at[n])
        for n, (a, b) in enumerate((
            (k_hbm, kv.at[z, c, 0]),
            (v_hbm, kv.at[z, c, 1]),
            (table_hbm, table),
            (dq_hbm, dq_in),
            (nk_hbm, nk_in),
            (nv_hbm, nv_in),
            (lens_hbm, lens),
            (ck_hbm, ck),
            (cv_hbm, cv),
            (q_hbm, qv.at[0]),
            (w_hbm, wv.at[xh, c]),
        ))
    ]
    for load in loads:
        load.start()
    barrier = pltpu.get_barrier_semaphore()

    def greet(o, _):
        to = lax.rem(here + o, plane)
        pl.semaphore_signal(barrier, inc=1, device_id=(z * 4 + to % 4, to // 4), device_id_type=MESH)
        return 0

    for d in (0, 1):
        pl.semaphore_signal(barrier, inc=1, device_id=toward(d), device_id_type=MESH)
    lax.fori_loop(1, plane, greet, 0)
    loads[0].wait()
    loads[1].wait()
    pl.semaphore_wait(barrier, plane + 1)

    def along(d, p, s, zb):
        ref = kv.at[zb, c, p]
        return move(ref, ref, zs.at[d, p, s - 1], zr.at[d, p, s - 1], toward(d))

    def over(d, s, cc):
        ref = kv.at[block(d, s), cc]
        return move(ref, ref, ss.at[d, s - 1], sr.at[d, s - 1], sibling)

    def over_own(cc):
        ref = kv.at[z, cc]
        return move(ref, ref, os, orr, sibling)

    every = [(p, d) for p in (0, 1) for d in (0, 1)]
    for p, d in every:
        along(d, p, 1, z).start()
    over_own(c).start()

    for load in loads[2:4]:
        load.wait()
    for r in range(4):
        dq32[pl.ds(r * STEPS, STEPS), :] = dq_in[r].astype(F32)
    line = dq32[...].astype(BF16)
    for h in range(GROUP):
        dqs[0, h * lines:(h + 1) * lines] = line[:, h * HD:(h + 1) * HD]

    page_row = lax.broadcasted_iota(jnp.int32, flags.shape[1:], 0)
    page_col = lax.broadcasted_iota(jnp.int32, flags.shape[1:], 1)
    page_id = jnp.where(page_col < 32, page_row * 32 + page_col, -1)

    def flag(slot, found):
        return jnp.where(page_id == table[0, slot], 1.0, found)

    flags[0] = lax.fori_loop(0, slots, flag, jnp.zeros(flags.shape[1:], F32), unroll=8)

    def swap(n, src, dst):
        return move(src, dst, xs.at[n], xr.at[n], beside)

    swaps = [
        swap(0, dqs.at[0], dqs.at[1]),
        swap(1, flags.at[0], flags.at[1]),
        swap(2, q_hbm, qv.at[1]),
        swap(3, ob.at[0], ob.at[1]),
        swap(4, ost.at[0], ost.at[1]),
        swap(5, db.at[0], db.at[1]),
        swap(6, dst.at[0], dst.at[1]),
    ]

    def weight(n, xx, source, to):
        return move(source, wv.at[xx, c], ws.at[n], wr.at[n], to)

    weights_out = [
        weight(0, xh, w_hbm, sibling),
        weight(1, xh, w_hbm, beside),
        weight(2, 1 - xh, wv.at[1 - xh, c], sibling),
    ]

    def weight_in(n, xx, cc):
        ref = wv.at[xx, cc]
        return move(ref, ref, ws.at[n], wr.at[n], sibling)

    for n in range(3):
        swaps[n].start()
    for n in range(2):
        weights_out[n].start()

    def own_decode():
        for load in loads[4:9]:
            load.wait()
        nk32[...] = jnp.zeros_like(nk32)
        nv32[...] = jnp.zeros_like(nv32)
        for r in range(4):
            nk32[pl.ds(r * STEPS, STEPS), :] = nk_in[r].astype(F32)
            nv32[pl.ds(r * STEPS, STEPS), :] = nv_in[r].astype(F32)
        queries = dqs[0]
        q_id = lax.broadcasted_iota(jnp.int32, (rows, cache), 0)
        k_id = lax.broadcasted_iota(jnp.int32, (rows, cache), 1)
        q_row = (q_id >> 2) & 3
        scores = []
        for r in range(4):
            live = (q_row == r) & (k_id < lens[r])
            scores.append(jnp.where(live, dot_t(queries, ck[r]), NEGATIVE))
        n_id = lax.broadcasted_iota(jnp.int32, (rows, HD), 0)
        u_id = lax.broadcasted_iota(jnp.int32, (rows, HD), 1)
        live = ((u_id >> 2) == ((n_id >> 2) & 3)) & ((u_id & 3) <= (n_id & 3))
        scores.append(jnp.where(live, dot_t(queries, nk32[...].astype(BF16)), NEGATIVE))
        most = row_max(scores[-1])
        for r in range(4):
            most = jnp.maximum(most, row_max(scores[r]))
        total = jnp.zeros((rows, 2 * HD), F32)
        for r in range(4):
            weights = jnp.exp2((scores[r] - wide(most, cache // HD)) * SCALE)
            total += dot(weights.astype(BF16), with_ones(cv[r]))
        weights = jnp.exp2((scores[-1] - most) * SCALE)
        total += dot(weights.astype(BF16), with_ones(nv32[...].astype(BF16)))
        dacc[0:rows] = total
        dtop[0:rows] = most
        dacc[rows:] = jnp.zeros((rows, 2 * HD), F32)
        dtop[rows:] = jnp.full((rows, HD), NEGATIVE, F32)

    def page_bias():
        span = 2 * tokens
        lane = lax.broadcasted_iota(jnp.int32, (HD, span), 0)
        key = lax.broadcasted_iota(jnp.int32, (HD, span), 1)
        spread = (lane == xh * 16 + (key >> 4)).astype(F32).astype(BF16)
        for n in (0, 1):
            named = dot(flags[n].astype(BF16), spread)
            penalty = jnp.where(named > 0.5, 0.0, NEGATIVE)
            for zz in range(nz):
                bias[n, zz] = jnp.broadcast_to(penalty[zz:zz + 1], (8, span))

    def tall(a, n):
        return jnp.concatenate([a] * n, axis=0)

    def keys_of(blocks):
        return jnp.concatenate([kv[zb, cc, 0] for zb in blocks for cc in (0, 1)], axis=0)

    def values_of(blocks):
        return with_ones(jnp.concatenate([kv[zb, cc, 1] for zb in blocks for cc in (0, 1)], axis=0))

    def decode_step(blocks):
        queries = jnp.concatenate([dqs[0], dqs[1]], axis=0)
        scores = dot_t(queries, keys_of(blocks))
        penalty = jnp.concatenate(
            [
                jnp.concatenate([tall(bias[n, zb], rows // 8) for n in (0, 1)], axis=0)
                for zb in blocks
            ],
            axis=1,
        )
        scores = scores + penalty
        old = dtop[...]
        most = jnp.maximum(old, row_max(scores))
        weights = jnp.exp2((scores - wide(most, scores.shape[1] // HD)) * SCALE)
        dacc[...] = dacc[...] * wide(jnp.exp2((old - most) * SCALE), 2) + dot(
            weights.astype(BF16), values_of(blocks)
        )
        dtop[...] = most

    pairs = GROUP // 2

    def attend(side, zb, masked):
        keys = keys_of([zb])
        values = values_of([zb])
        live = None
        if masked:
            q_id = lax.broadcasted_iota(jnp.int32, (2 * tokens, 2 * tokens), 0) & (tokens - 1)
            k_id = lax.broadcasted_iota(jnp.int32, (2 * tokens, 2 * tokens), 1)
            live = k_id <= c * tokens + q_id
        for pair in range(pairs):
            first = 2 * pair * HD
            q2 = jnp.concatenate(
                [qv[side, :, first:first + HD], qv[side, :, first + HD:first + 2 * HD]], axis=0
            )
            scores = dot_t(q2, keys)
            place = side * pairs + pair
            if masked:
                scores = jnp.where(live, scores, NEGATIVE)
                most = row_max(scores)
            else:
                old = top[place]
                most = jnp.maximum(old, row_max(scores))
            weights = jnp.exp2((scores - wide(most, 2 * tokens // HD)) * SCALE)
            mixed = dot(weights.astype(BF16), values)
            if not masked:
                mixed += acc[place] * wide(jnp.exp2((old - most) * SCALE), 2)
            acc[place] = mixed
            top[place] = most

    def attend_pair(side, s):
        def one(d, _):
            @pl.when(jnp.where(d == 0, z - s >= 0, z + s >= nz))
            def _():
                attend(side, block(d, s), False)

            return 0

        lax.fori_loop(0, 2, one, 0)

    early = 2 if half >= 4 else 0

    def attend_number(n):
        side = jnp.where((n >= early) & (n < early + half - 1), 1, 0)
        s = jnp.where(n < early, n + 1, jnp.where(side == 1, n - early + 1, n - half + 2))
        attend_pair(side, s)

    def ring(s, _):
        for p, d in every:
            zb = block(d, s)
            along(d, p, s, zb).wait_recv()
            if p == d:
                along(d, p, s + 1, zb).start()
            else:
                @pl.when(s < half - 1)
                def _():
                    along(d, p, s + 1, zb).start()
            if p == 1:
                over(d, s, c).start()

        @pl.when(s == 1)
        def _():
            own_decode()
            loads[9].wait()
            over_own(1 - c).wait_recv()
            attend(0, z, True)
            swaps[0].wait_recv()
            swaps[1].wait_recv()
            page_bias()
            decode_step([z])
            acc[pairs:] = jnp.zeros((pairs, 2 * tokens, 2 * HD), F32)
            top[pairs:] = jnp.full((pairs, 2 * tokens, HD), NEGATIVE, F32)

        @pl.when(s > 1)
        def _():
            for d in (0, 1):
                over(d, s - 1, 1 - c).wait_recv()
            decode_step([block(0, s - 1), block(1, s - 1)])

            @pl.when(s == early + 2)
            def _():
                swaps[2].wait_recv()

            attend_number(s - 2)

        return 0

    lax.fori_loop(1, half, ring, 0)
    if half - 1 < early + 2:
        swaps[2].wait_recv()
    for d in (0, 1):
        over(d, half - 1, 1 - c).wait_recv()
    decode_step([block(0, half - 1), block(1, half - 1)])
    weights_out[1].wait_recv()
    weights_out[2].start()
    for d in (0, 1):
        along(d, d, half, block(d, half)).wait_recv()
    over(0, half, c).start()
    over(0, half, 1 - c).wait_recv()
    decode_step([block(0, half)])

    eye = lax.broadcasted_iota(jnp.int32, (HD, HD), 0) == lax.broadcasted_iota(jnp.int32, (HD, HD), 1)

    def flat(a):
        return jnp.sum(jnp.where(eye, a, 0.0), axis=0, keepdims=True)

    def upright(a):
        return jnp.transpose(jnp.broadcast_to(a, (HD, HD)))

    def part(total, most):
        weight_sum = jnp.maximum(total[:, HD:], 1e-30)
        return (total[:, :HD] / weight_sum).astype(BF16), most * SCALE + jnp.log2(weight_sum)

    def join(total, most, other, level):
        level_own = most * SCALE
        high = jnp.maximum(level_own, level)
        own, far = jnp.exp2(level_own - high), jnp.exp2(level - high)
        return (total[:, :HD] * own + other.astype(F32) * far) / (total[:, HD:] * own + far)

    out, level = part(dacc[rows:], dtop[rows:])
    db[0] = out
    dst[0] = jnp.broadcast_to(flat(level), (8, HD))
    swaps[5].start()
    swaps[6].start()
    swaps[5].wait_recv()
    swaps[6].wait_recv()
    mixed = join(dacc[0:rows], dtop[0:rows], db[1], upright(dst[1, 0:1])).astype(BF16)
    for h in range(GROUP):
        att[z, h // 4, h % 4] = mixed[h * lines:(h + 1) * lines]

    def share(d, s, zb):
        return move(att.at[zb], att.at[zb], at_s.at[d, s - 1], at_r.at[d, s - 1], toward(d))

    def share_half(d, zb):
        ref = att.at[zb, d]
        return move(ref, ref, at_s.at[d, half - 1], at_r.at[d, half - 1], toward(d))

    for d in (0, 1):
        share(d, 1, z).start()

    def send_parts():
        @pl.when(xh == 0)
        def _():
            attend(1, z, False)

        @pl.when(z >= half)
        def _():
            attend(1, block(0, half), False)

        for pair in range(pairs):
            out, level = part(acc[pairs + pair], top[pairs + pair])
            ob[0, pair] = out
            for n in (0, 1):
                ost[0, 2 * pair + n:2 * pair + n + 1] = flat(level[n * tokens:(n + 1) * tokens])
        swaps[3].start()
        swaps[4].start()

    def pass_on(s, _):
        for d in (0, 1):
            zb = block(d, s)
            share(d, s, zb).wait_recv()

            @pl.when(s < half - 1)
            def _():
                share(d, s + 1, zb).start()

            @pl.when(s == half - 1)
            def _():
                share_half(d, zb).start()

        attend_number(half - 3 + s)

        @pl.when(s == early + 1)
        def _():
            send_parts()

        return 0

    lax.fori_loop(1, half, pass_on, 0)
    attend_number(2 * half - 3)
    weight_in(0, xh, 1 - c).wait_recv()
    weight_in(2, 1 - xh, 1 - c).wait_recv()
    loads[10].wait()
    for d in (0, 1):
        share_half(d, block(d, half)).wait_recv()

    lhs = jnp.concatenate(
        [att[:, h // 4, h % 4].reshape(nz * lines, HD) for h in range(GROUP)], axis=1
    )
    depth = sbuf.shape[2]
    for xx in (0, 1):
        term = dot(lhs, jnp.concatenate([wv[xx, 0], wv[xx, 1]], axis=1)).astype(BF16)
        for cc in (0, 1):
            for j in range(ntp):
                sbuf[j, xx * 2 + cc] = term[j * depth:(j + 1) * depth, cc * HD:(cc + 1) * HD]

    def deal(o, to, source):
        return move(
            sbuf.at[to // 4, to % 4],
            rbuf.at[source // 4, source % 4],
            rs.at[o - 1],
            rr.at[o - 1],
            (z * 4 + to % 4, to // 4),
        )

    def deal_out(o, _):
        deal(o, lax.rem(here + o, plane), here).start()
        return 0

    lax.fori_loop(1, plane, deal_out, 0)
    rbuf[tp, mine] = sbuf[tp, mine]

    @pl.when(z >= half)
    def _():
        attend(0, block(0, half), False)

    swaps[3].wait_recv()
    swaps[4].wait_recv()
    for pair in range(pairs):
        level = jnp.concatenate(
            [upright(ost[1, 2 * pair + n:2 * pair + n + 1]) for n in (0, 1)], axis=0
        )
        out = join(acc[pair], top[pair], ob[1, pair], level).astype(BF16)
        for n in (0, 1):
            first = (2 * pair + n) * HD
            prev[:, first:first + HD] = out[n * tokens:(n + 1) * tokens]
    store_pre = pltpu.make_async_copy(prev, pre_hbm, loc.at[11])
    store_pre.start()

    def deal_in(o, _):
        deal(o, lax.rem(here + o, plane), lax.rem(here + plane - o, plane)).wait_recv()
        return 0

    lax.fori_loop(1, plane, deal_in, 0)
    for n in range(4):
        total = rbuf[0, n].astype(F32)
        for j in range(1, ntp):
            total += rbuf[j, n].astype(F32)
        total = total.astype(BF16)
        for zz in range(depth // lines):
            first = (zz * 4 + n) * lines
            decv[first:first + lines] = total[zz * lines:(zz + 1) * lines]
    store_dec = pltpu.make_async_copy(decv, dec_hbm, loc.at[12])
    store_dec.start()

    def ring_sent(s, _):
        for p, d in every:
            along(d, p, s, block(d, s - 1)).wait_send()
        for d in (0, 1):
            over(d, s, c).wait_send()
            share(d, s, block(d, s - 1)).wait_send()
        return 0

    lax.fori_loop(1, half, ring_sent, 0)
    for d in (0, 1):
        along(d, d, half, block(d, half - 1)).wait_send()
        share_half(d, block(d, half - 1)).wait_send()
    over(0, half, c).wait_send()
    over_own(c).wait_send()
    for copy in swaps + weights_out:
        copy.wait_send()

    def dealt(o, _):
        deal(o, lax.rem(here + o, plane), here).wait_send()
        return 0

    lax.fori_loop(1, plane, dealt, 0)
    store_pre.wait()
    store_dec.wait()


def local(pre_q, pre_k, pre_v, page_table, dec_q, dec_new_k, dec_new_v, cache_k, cache_v, cache_len, out_weight):
    nz = lax.axis_size("ctx") // 4
    ntp = lax.axis_size("tp")
    half = nz // 2
    tokens, width = pre_q.shape
    row_dev, cache = cache_k.shape[:2]
    lines = row_dev * STEPS
    rows = GROUP * lines
    plane = 4 * ntp
    out_rows = nz * 4 * lines // ntp
    depth = nz // ntp * lines
    hbm = pl.BlockSpec(memory_space=pltpu.HBM)
    sem = pltpu.SemaphoreType.DMA

    def vmem(shape, dtype=BF16):
        return pltpu.VMEM(shape, dtype)

    return pl.pallas_call(
        functools.partial(kernel, nz, ntp),
        out_shape=(
            jax.ShapeDtypeStruct((tokens, width), BF16),
            jax.ShapeDtypeStruct((out_rows, HD), BF16),
        ),
        in_specs=[hbm] * 11,
        out_specs=(hbm, hbm),
        scratch_shapes=[
            pltpu.SMEM(page_table.shape, jnp.int32),
            pltpu.SMEM(cache_len.shape, jnp.int32),
            vmem(dec_q.shape),
            vmem(dec_new_k.shape),
            vmem(dec_new_v.shape),
            vmem((nz, 2, 2, tokens, HD)),
            vmem((2, tokens, width)),
            vmem((row_dev, cache, HD)),
            vmem((row_dev, cache, HD)),
            vmem((2, 2, width, HD)),
            vmem((GROUP, 2 * tokens, 2 * HD), F32),
            vmem((GROUP, 2 * tokens, HD), F32),
            vmem((lines, width), F32),
            vmem((HD, HD), F32),
            vmem((HD, HD), F32),
            vmem((2, rows, HD)),
            vmem((2, -(-nz // 8) * 8, HD), F32),
            vmem((2, nz, 8, 2 * tokens), F32),
            vmem((2 * rows, 2 * HD), F32),
            vmem((2 * rows, HD), F32),
            vmem((2, GROUP // 2, 2 * tokens, HD)),
            vmem((2, GROUP, HD), F32),
            vmem((2, rows, HD)),
            vmem((2, 8, HD), F32),
            vmem((nz, 2, 4, lines, HD)),
            vmem((ntp, 4, depth, HD)),
            vmem((ntp, 4, depth, HD)),
            vmem((tokens, width)),
            vmem((out_rows, HD)),
            sem((13,)),
            sem((2, 2, half)), sem((2, 2, half)),
            sem((2, half)), sem((2, half)),
            sem(()), sem(()),
            sem((7,)), sem((7,)),
            sem((3,)), sem((3,)),
            sem((2, half)), sem((2, half)),
            sem((plane - 1,)), sem((plane - 1,)),
        ],
        compiler_params=pltpu.CompilerParams(
            collective_id=0, has_side_effects=True, vmem_limit_bytes=63 << 20
        ),
    )(
        pre_q, pre_k, pre_v, page_table, dec_q, dec_new_k, dec_new_v, cache_k, cache_v, cache_len, out_weight
    )


def solution(mesh):
    placed = (
        P("ctx", "tp"),
        P("ctx", "tp"),
        P("ctx", "tp"),
        P("ctx", None),
        P("ctx", None, "tp"),
        P("ctx", None, "tp"),
        P("ctx", None, "tp"),
        P("ctx", None, "tp"),
        P("ctx", None, "tp"),
        P("ctx"),
        P("tp", "ctx"),
    )
    return jax.shard_map(
        local,
        mesh=mesh,
        in_specs=placed,
        out_specs=(P("ctx", "tp"), P("tp", "ctx")),
        check_vma=False,
    )
```

```python
import functools
import math

import jax
import jax.numpy as jnp
from jax import lax
from jax.experimental import pallas as pl
from jax.experimental.pallas import tpu as pltpu
from jax.sharding import PartitionSpec as P

MESH = pl.DeviceIdType.MESH
HD = 128
GROUP = 8
STEPS = 4
EXTRA = 16
NEGATIVE = -1e30
SCALE = HD ** -0.5 * math.log2(math.e)
F32 = jnp.float32
BF16 = jnp.bfloat16


def dot_t(a, b):
    return lax.dot_general(a, b, (((1,), (1,)), ((), ())), preferred_element_type=F32)


def dot(a, b):
    return jnp.dot(a, b, preferred_element_type=F32)


def wide(a, n):
    return jnp.concatenate([a] * n, axis=1)


def with_ones(values):
    return jnp.concatenate([values, jnp.ones(values.shape, BF16)], axis=1)


def row_max(scores):
    top = jnp.max(scores, axis=1, keepdims=True)
    return jnp.broadcast_to(top, (scores.shape[0], HD))


def kernel(
    nz, ntp,
    q_hbm, k_hbm, v_hbm, table_hbm, dq_hbm, nk_hbm, nv_hbm, ck_hbm, cv_hbm, lens_hbm, w_hbm,
    pre_hbm, dec_hbm,
    lens, tab_in, v_in, q_in, dq_in, nk_in, nv_in,
    kv, qt, ck, cv, wv, acc, top, dq32, nk32, nv32, dqs, dqt, tabs, bias, dacc, dtop,
    ob, ost, db, dst, att, sbuf, rbuf, mbuf, fbuf, prev, decv,
    loc, zs, zr, ss, sr, os, orr, xs, xr, ws, wr, at_s, at_r, rs, rr, bs, br,
):
    half = nz // 2
    rounds = half // 2
    ctx = lax.axis_index("ctx")
    tp = lax.axis_index("tp")
    z, xh, c = ctx // 4, (ctx // 2) % 2, ctx % 2
    mine = ctx % 4
    tokens = q_in.shape[0]
    cache = ck.shape[1]
    slots = tab_in.shape[1]
    lines = dq32.shape[0]
    rows = GROUP * lines

    def turned(a):
        return jnp.transpose(a.astype(F32))

    def device(zz, xx, cc):
        return (zz * 4 + xx * 2 + cc, tp)

    def move(src, dst, send, recv, to):
        return pltpu.make_async_remote_copy(
            src_ref=src, dst_ref=dst, send_sem=send, recv_sem=recv, device_id=to, device_id_type=MESH
        )

    sibling = device(z, xh, 1 - c)
    beside = device(z, 1 - xh, c)
    across = device(z, 1 - xh, 1 - c)

    def toward(d, hops):
        return device(lax.rem(z + (hops if d == 0 else nz - hops), nz), xh, c)

    def block(d, s):
        return lax.rem(jnp.where(d == 0, z + nz - s, z + s), nz)

    loads = [
        pltpu.make_async_copy(a, b, loc.at[n])
        for n, (a, b) in enumerate((
            (k_hbm, kv.at[z, c, 0]),
            (v_hbm, v_in),
            (table_hbm, tab_in),
            (dq_hbm, dq_in),
            (nk_hbm, nk_in),
            (nv_hbm, nv_in),
            (lens_hbm, lens),
            (ck_hbm, ck),
            (cv_hbm, cv),
            (q_hbm, q_in),
            (w_hbm, wv.at[xh, c]),
        ))
    ]
    for load in loads:
        load.start()
    barrier = pltpu.get_barrier_semaphore()

    def greet(o, _):
        pl.semaphore_signal(barrier, inc=1, device_id=(ctx, lax.rem(tp + o, ntp)), device_id_type=MESH)
        return 0

    along_z = [toward(d, hops) for hops in (1, 2, 3) for d in (0, 1)]
    for to in along_z + [sibling, beside, across]:
        pl.semaphore_signal(barrier, inc=1, device_id=to, device_id_type=MESH)
    lax.fori_loop(1, ntp, greet, 0)
    loads[0].wait()
    loads[1].wait()
    kv[z, c, 1] = turned(v_in[...]).astype(BF16)
    pl.semaphore_wait(barrier, ntp + 8)

    def along(d, p, s, zb):
        ref = kv.at[zb, c, p]
        to = toward(d, 2 - s % 2)
        return move(ref, ref, zs.at[d, p, s - 1], zr.at[d, p, s - 1], to)

    def over(d, s, cc):
        ref = kv.at[block(d, s), cc]
        return move(ref, ref, ss.at[d, s - 1], sr.at[d, s - 1], sibling)

    def over_own(cc):
        ref = kv.at[z, cc]
        return move(ref, ref, os, orr, sibling)

    every = [(p, d) for p in (0, 1) for d in (0, 1)]
    for p, d in every:
        if rounds > 1 or p == d:
            along(d, p, 2, z).start()
    for p, d in every:
        along(d, p, 1, z).start()
    over_own(c).start()

    for load in loads[2:4]:
        load.wait()
    tabs[0] = jnp.full(tabs.shape[1:], -1, jnp.int32)
    tabs[0, 0:1, 0:slots] = tab_in[...]
    for r in range(4):
        dq32[pl.ds(r * STEPS, STEPS), :] = dq_in[r].astype(F32)
    line = dq32[...]
    stacked = jnp.concatenate([line[:, h * HD:(h + 1) * HD] for h in range(GROUP)], axis=0)
    dqs[...] = stacked.astype(BF16)
    dqt[0] = jnp.transpose(stacked).astype(BF16)

    def swap(n, src, dst):
        return move(src, dst, xs.at[n], xr.at[n], beside)

    swaps = [
        swap(0, dqt.at[0], dqt.at[1]),
        swap(1, tabs.at[0], tabs.at[1]),
        swap(2, qt.at[0], qt.at[1]),
        swap(3, ob.at[0], ob.at[1]),
        swap(4, ost.at[0], ost.at[1]),
        swap(5, db.at[0], db.at[1]),
        swap(6, dst.at[0], dst.at[1]),
    ]

    def weight(n, xx, source, to):
        return move(source, wv.at[xx, c], ws.at[n], wr.at[n], to)

    weights_out = [
        weight(0, xh, w_hbm, sibling),
        weight(1, xh, w_hbm, beside),
        weight(2, 1 - xh, wv.at[1 - xh, c], sibling),
    ]

    def weight_in(n, xx, cc):
        ref = wv.at[xx, cc]
        return move(ref, ref, ws.at[n], wr.at[n], sibling)

    for n in range(2):
        swaps[n].start()
    loads[9].wait()
    for h in range(GROUP):
        qt[0, :, h * HD:(h + 1) * HD] = turned(q_in[:, h * HD:(h + 1) * HD]).astype(BF16)
    swaps[2].start()
    for n in range(2):
        weights_out[n].start()

    def own_decode():
        for load in loads[4:9]:
            load.wait()
        nk32[...] = jnp.zeros_like(nk32)
        nv32[...] = jnp.zeros_like(nv32)
        for r in range(4):
            nk32[pl.ds(r * STEPS, STEPS), :] = nk_in[r].astype(F32)
            nv32[pl.ds(r * STEPS, STEPS), :] = nv_in[r].astype(F32)
        queries = dqs[...]
        q_id = lax.broadcasted_iota(jnp.int32, (rows, cache), 0)
        k_id = lax.broadcasted_iota(jnp.int32, (rows, cache), 1)
        q_row = (q_id >> 2) & 3
        scores = []
        for r in range(4):
            live = (q_row == r) & (k_id < lens[r])
            scores.append(jnp.where(live, dot_t(queries, ck[r]), NEGATIVE))
        n_id = lax.broadcasted_iota(jnp.int32, (rows, HD), 0)
        u_id = lax.broadcasted_iota(jnp.int32, (rows, HD), 1)
        live = ((u_id >> 2) == ((n_id >> 2) & 3)) & ((u_id & 3) <= (n_id & 3))
        scores.append(jnp.where(live, dot_t(queries, nk32[...].astype(BF16)), NEGATIVE))
        most = row_max(scores[-1])
        for r in range(4):
            most = jnp.maximum(most, row_max(scores[r]))
        total = jnp.zeros((rows, 2 * HD), F32)
        for r in range(4):
            weights = jnp.exp2((scores[r] - wide(most, cache // HD)) * SCALE)
            total += dot(weights.astype(BF16), with_ones(cv[r]))
        weights = jnp.exp2((scores[-1] - most) * SCALE)
        total += dot(weights.astype(BF16), with_ones(nv32[...].astype(BF16)))
        dacc[0:HD, 0:rows] = jnp.transpose(total[:, :HD])
        dacc[HD:, 0:rows] = jnp.transpose(total[:, HD:])[0:EXTRA]
        dtop[0:1, 0:rows] = jnp.transpose(most)[0:1]
        dacc[:, rows:] = jnp.zeros((HD + EXTRA, rows), F32)
        dtop[0:1, rows:] = jnp.full((1, rows), NEGATIVE, F32)

    def page_bias():
        line_id = lax.broadcasted_iota(jnp.int32, (nz * 16, HD), 0)
        page = (line_id >> 4) * 32 + xh * 16 + (line_id & 15)
        for n in (0, 1):
            named = jnp.where(page == tabs[n, 0:1], 1.0, 0.0)
            found = jnp.max(named, axis=1, keepdims=True)
            penalty = jnp.broadcast_to(jnp.where(found > 0.5, 0.0, NEGATIVE), (nz * 16, HD))
            bias[:, :, n * HD:(n + 1) * HD] = penalty.reshape(nz, 16, HD)

    def keys_of(blocks):
        return jnp.concatenate([kv[zb, cc, 0] for zb in blocks for cc in (0, 1)], axis=0)

    def values_of(blocks):
        values = jnp.concatenate([kv[zb, cc, 1] for zb in blocks for cc in (0, 1)], axis=1)
        return jnp.concatenate([values, jnp.ones((EXTRA, values.shape[1]), BF16)], axis=0)

    def update(scores, old, total, values):
        most = jnp.max(scores, axis=0, keepdims=True)
        if old is not None:
            most = jnp.maximum(old, most)
        weights = jnp.exp2((scores - most) * SCALE).astype(BF16)
        mixed = dot(values, weights)
        if old is not None:
            mixed += total * jnp.exp2((old - most) * SCALE)
        return most, mixed

    def decode_step(blocks):
        queries = jnp.concatenate([dqt[0], dqt[1]], axis=1)
        scores = dot(keys_of(blocks), queries)
        penalty = []
        for zb in blocks:
            lines_of = bias[zb]
            penalty += [jnp.broadcast_to(lines_of[n:n + 1], (16, 2 * rows)) for n in range(16)]
        scores = scores + jnp.concatenate(penalty, axis=0)
        most, mixed = update(scores, dtop[0:1], dacc[...], values_of(blocks))
        dacc[...] = mixed
        dtop[0:1] = most

    lanes = [slice(n, n + 2 * HD) for n in range(0, GROUP * HD, 2 * HD)]

    def attend(side, blocks, masked):
        keys = keys_of(blocks)
        values = values_of(blocks)
        scores = [dot(keys, qt[side, :, cols]) for cols in lanes]
        if masked:
            k_id = lax.broadcasted_iota(jnp.int32, (2 * tokens, 2 * HD), 0)
            q_id = lax.broadcasted_iota(jnp.int32, (2 * tokens, 2 * HD), 1) & (tokens - 1)
            live = k_id <= c * tokens + q_id
            done = [
                update(jnp.where(live, part_scores, NEGATIVE), None, None, values)
                for part_scores in scores
            ]
        else:
            done = [
                update(part_scores, top[side, 0:1, cols], acc[side, :, cols], values)
                for part_scores, cols in zip(scores, lanes)
            ]
        for (most, mixed), cols in zip(done, lanes):
            acc[side, :, cols] = mixed
            top[side, 0:1, cols] = most

    def attend_some(side, first, second, one, both):
        @pl.when(both)
        def _():
            attend(side, [first, second], False)

        @pl.when(one & jnp.logical_not(both))
        def _():
            attend(side, [first], False)

    early = 3 if half >= 8 else 0

    def numbered(n):
        side = jnp.where((n >= early) & (n < early + half - 1), 1, 0)
        s = jnp.where(n < early, n + 1, jnp.where(side == 1, n - early + 1, n - half + 2))
        return side, block(0, s), block(1, s), z >= s, z + s >= nz

    total_pairs = 2 * (half - 1)
    first_partner = early // 2 + 2

    def attend_range(start, stop):
        def one(n, _):
            attend_some(*numbered(n))
            return 0

        lax.fori_loop(start, stop, one, 0)

    own_decode()
    over_own(1 - c).wait_recv()
    attend(0, [z], True)
    acc[1] = jnp.zeros(acc.shape[1:], F32)
    top[1, 0:1] = jnp.full((1, GROUP * HD), NEGATIVE, F32)
    swaps[0].wait_recv()
    swaps[1].wait_recv()
    page_bias()
    decode_step([z])

    def ring(k, _):
        for p, d in every:
            zb = block(d, 2 * k - 2)
            along(d, p, 2 * k - 2, zb).wait_recv()
            if p == d:
                along(d, p, 2 * k, zb).start()
            else:
                @pl.when(k < rounds)
                def _():
                    along(d, p, 2 * k, zb).start()
        for p, d in every:
            along(d, p, 2 * k - 1, block(d, 2 * k - 2)).start()
        for d in (0, 1):
            over(d, 2 * k - 2, c).start()
        for p, d in every:
            along(d, p, 2 * k - 3, block(d, 2 * k - 3)).wait_recv()
        for d in (0, 1):
            over(d, 2 * k - 3, c).start()
        for s in (2 * k - 2, 2 * k - 3):
            for d in (0, 1):
                over(d, s, 1 - c).wait_recv()
        decode_step([block(d, s) for s in (2 * k - 3, 2 * k - 2) for d in (0, 1)])

        @pl.when(k == first_partner)
        def _():
            swaps[2].wait_recv()

        attend_range(2 * k - 4, 2 * k - 2)
        return 0

    lax.fori_loop(2, rounds + 1, ring, 0)
    if rounds < first_partner:
        swaps[2].wait_recv()
    weights_out[1].wait_recv()
    weights_out[2].start()
    for d in (0, 1):
        along(d, d, half, block(d, half)).wait_recv()
    over(0, half, c).start()
    for p, d in every:
        along(d, p, half - 1, block(d, half - 1)).wait_recv()
    for d in (0, 1):
        over(d, half - 1, c).start()
    over(0, half, 1 - c).wait_recv()
    for d in (0, 1):
        over(d, half - 1, 1 - c).wait_recv()
    decode_step([block(0, half - 1), block(1, half - 1), block(0, half)])

    def part(total, most):
        weight_sum = jnp.maximum(total[HD:HD + 1], 1e-30)
        return (total[:HD] / weight_sum).astype(BF16), most * SCALE + jnp.log2(weight_sum)

    def join(total, most, other, level):
        level_own = most * SCALE
        high = jnp.maximum(level_own, level)
        own, far = jnp.exp2(level_own - high), jnp.exp2(level - high)
        scale = 1.0 / (total[HD:HD + 1] * own + far)
        return total[:HD] * (own * scale) + other.astype(F32) * (far * scale)

    out, level = part(dacc[:, rows:], dtop[0:1, rows:])
    db[0] = out
    dst[0] = jnp.broadcast_to(level, (8, HD))
    swaps[5].start()
    swaps[6].start()
    done_pairs = 2 * (rounds - 1)
    attend_range(done_pairs, min(done_pairs + 2, total_pairs))
    done_pairs = min(done_pairs + 2, total_pairs)
    swaps[5].wait_recv()
    swaps[6].wait_recv()
    mixed = jnp.transpose(join(dacc[:, 0:rows], dtop[0:1, 0:rows], db[1], dst[1, 0:1])).astype(BF16)
    for h in range(GROUP):
        att[z, h // 4, h % 4] = mixed[h * lines:(h + 1) * lines]

    reach = 3

    def share(d, s, zb):
        ref = att.at[zb] if s < half else att.at[zb, d]
        to = toward(d, (s - 1) % reach + 1)
        return move(ref, ref, at_s.at[d, s - 1], at_r.at[d, s - 1], to)

    def spread(base):
        for s in range(min(base + reach, half), base, -1):
            for d in (0, 1):
                share(d, s, block(d, base)).start()

    def send_parts():
        def more(j, _):
            first = jnp.where(j == 0, z, block(0, half))
            attend_some(1, first, first, jnp.where(j == 0, 1 - xh, z // half) > 0, j < 0)
            return 0

        lax.fori_loop(0, 2, more, 0)
        out, level = part(acc[1], top[1, 0:1])
        ob[0] = out
        ost[0] = jnp.broadcast_to(level, (8, GROUP * HD))
        swaps[3].start()
        swaps[4].start()

    bases = list(range(0, half, reach))
    for base in bases:
        if base:
            for d in (0, 1):
                share(d, base, block(d, base)).wait_recv()
        spread(base)
        stop = total_pairs if base == bases[-1] else min(done_pairs + 2, total_pairs)
        if done_pairs < stop:
            attend_range(done_pairs, stop)
        done_pairs = stop
        if base == 0:
            send_parts()
    weight_in(0, xh, 1 - c).wait_recv()
    weight_in(2, 1 - xh, 1 - c).wait_recv()
    loads[10].wait()
    for s in range(1, half + 1):
        if s not in bases:
            for d in (0, 1):
                share(d, s, block(d, s)).wait_recv()

    lhs = jnp.concatenate(
        [att[:, h // 4, h % 4].reshape(nz * lines, HD) for h in range(GROUP)], axis=1
    )
    depth = sbuf.shape[2]
    for xx in (0, 1):
        term = dot(lhs, jnp.concatenate([wv[xx, 0], wv[xx, 1]], axis=1)).astype(BF16)
        for cc in (0, 1):
            for j in range(ntp):
                sbuf[j, xx * 2 + cc] = term[j * depth:(j + 1) * depth, cc * HD:(cc + 1) * HD]

    def deal(o, to, source):
        return move(sbuf.at[to], rbuf.at[source], rs.at[o - 1], rr.at[o - 1], (ctx, to))

    def deal_out(o, _):
        deal(o, lax.rem(tp + o, ntp), tp).start()
        return 0

    lax.fori_loop(1, ntp, deal_out, 0)
    rbuf[tp] = sbuf[tp]

    def deal_in(o, _):
        deal(o, lax.rem(tp + o, ntp), lax.rem(tp + ntp - o, ntp)).wait_recv()
        return 0

    lax.fori_loop(1, ntp, deal_in, 0)
    total = rbuf[0].astype(F32)
    for j in range(1, ntp):
        total += rbuf[j].astype(F32)
    mbuf[...] = total.astype(BF16)
    near = ((sibling, xh, 1 - c), (beside, 1 - xh, c), (across, 1 - xh, 1 - c))

    def hand(n):
        to, xx, cc = near[n]
        return move(mbuf.at[xx * 2 + cc], fbuf.at[mine], bs.at[n], br.at[n], to)

    def handed(n):
        to, xx, cc = near[n]
        return move(mbuf.at[mine], fbuf.at[xx * 2 + cc], bs.at[n], br.at[n], to)

    for n in range(3):
        hand(n).start()
    fbuf[mine] = mbuf[mine]

    @pl.when(z >= half)
    def _():
        attend(0, [block(0, half)], False)

    swaps[3].wait_recv()
    swaps[4].wait_recv()
    whole = join(acc[0], top[0, 0:1], ob[1], ost[1, 0:1])
    for h in range(GROUP):
        prev[:, h * HD:(h + 1) * HD] = jnp.transpose(whole[:, h * HD:(h + 1) * HD]).astype(BF16)
    store_pre = pltpu.make_async_copy(prev, pre_hbm, loc.at[11])
    store_pre.start()

    for n in range(3):
        handed(n).wait_recv()
    for n in range(4):
        for zz in range(depth // lines):
            first = (zz * 4 + n) * lines
            decv[first:first + lines] = fbuf[n, zz * lines:(zz + 1) * lines]
    store_dec = pltpu.make_async_copy(decv, dec_hbm, loc.at[12])
    store_dec.start()

    def ring_sent(s, _):
        for p, d in every:
            along(d, p, s, block(d, (s - 1) // 2 * 2)).wait_send()
        for d in (0, 1):
            over(d, s, c).wait_send()
        return 0

    lax.fori_loop(1, half, ring_sent, 0)
    for s in range(1, half + 1):
        for d in (0, 1):
            share(d, s, block(d, (s - 1) // reach * reach)).wait_send()
    for d in (0, 1):
        along(d, d, half, block(d, half - 2)).wait_send()
    over(0, half, c).wait_send()
    over_own(c).wait_send()
    for copy in swaps + weights_out:
        copy.wait_send()

    for n in range(3):
        hand(n).wait_send()

    def dealt(o, _):
        deal(o, lax.rem(tp + o, ntp), tp).wait_send()
        return 0

    lax.fori_loop(1, ntp, dealt, 0)
    store_pre.wait()
    store_dec.wait()


def local(pre_q, pre_k, pre_v, page_table, dec_q, dec_new_k, dec_new_v, cache_k, cache_v, cache_len, out_weight):
    nz = lax.axis_size("ctx") // 4
    ntp = lax.axis_size("tp")
    half = nz // 2
    tokens, width = pre_q.shape
    row_dev, cache = cache_k.shape[:2]
    lines = row_dev * STEPS
    rows = GROUP * lines
    out_rows = nz * 4 * lines // ntp
    depth = nz // ntp * lines
    hbm = pl.BlockSpec(memory_space=pltpu.HBM)
    sem = pltpu.SemaphoreType.DMA

    def vmem(shape, dtype=BF16):
        return pltpu.VMEM(shape, dtype)

    return pl.pallas_call(
        functools.partial(kernel, nz, ntp),
        out_shape=(
            jax.ShapeDtypeStruct((tokens, width), BF16),
            jax.ShapeDtypeStruct((out_rows, HD), BF16),
        ),
        in_specs=[hbm] * 11,
        out_specs=(hbm, hbm),
        scratch_shapes=[
            pltpu.SMEM(cache_len.shape, jnp.int32),
            vmem(page_table.shape, jnp.int32),
            vmem((tokens, HD)),
            vmem((tokens, width)),
            vmem(dec_q.shape),
            vmem(dec_new_k.shape),
            vmem(dec_new_v.shape),
            vmem((nz, 2, 2, tokens, HD)),
            vmem((2, HD, width)),
            vmem((row_dev, cache, HD)),
            vmem((row_dev, cache, HD)),
            vmem((2, 2, width, HD)),
            vmem((2, HD + EXTRA, width), F32),
            vmem((2, 8, width), F32),
            vmem((lines, width), F32),
            vmem((HD, HD), F32),
            vmem((HD, HD), F32),
            vmem((rows, HD)),
            vmem((2, HD, rows)),
            vmem((2, 8, HD), jnp.int32),
            vmem((nz, 16, 2 * rows), F32),
            vmem((HD + EXTRA, 2 * rows), F32),
            vmem((8, 2 * rows), F32),
            vmem((2, HD, width)),
            vmem((2, 8, width), F32),
            vmem((2, HD, rows)),
            vmem((2, 8, HD), F32),
            vmem((nz, 2, 4, lines, HD)),
            vmem((ntp, 4, depth, HD)),
            vmem((ntp, 4, depth, HD)),
            vmem((4, depth, HD)),
            vmem((4, depth, HD)),
            vmem((tokens, width)),
            vmem((out_rows, HD)),
            sem((13,)),
            sem((2, 2, half)), sem((2, 2, half)),
            sem((2, half)), sem((2, half)),
            sem(()), sem(()),
            sem((7,)), sem((7,)),
            sem((3,)), sem((3,)),
            sem((2, half)), sem((2, half)),
            sem((max(ntp - 1, 1),)), sem((max(ntp - 1, 1),)),
            sem((3,)), sem((3,)),
        ],
        compiler_params=pltpu.CompilerParams(
            collective_id=0, has_side_effects=True, vmem_limit_bytes=63 << 20
        ),
    )(
        pre_q, pre_k, pre_v, page_table, dec_q, dec_new_k, dec_new_v, cache_k, cache_v, cache_len, out_weight
    )


def solution(mesh):
    placed = (
        P("ctx", "tp"),
        P("ctx", "tp"),
        P("ctx", "tp"),
        P("ctx", None),
        P("ctx", None, "tp"),
        P("ctx", None, "tp"),
        P("ctx", None, "tp"),
        P("ctx", None, "tp"),
        P("ctx", None, "tp"),
        P("ctx"),
        P("tp", "ctx"),
    )
    return jax.shard_map(
        local,
        mesh=mesh,
        in_specs=placed,
        out_specs=(P("ctx", "tp"), P("tp", "ctx")),
        check_vma=False,
    )
```

```python
import functools
import math

import jax
import jax.numpy as jnp
from jax import lax
from jax.experimental import pallas as pl
from jax.experimental.pallas import tpu as pltpu
from jax.sharding import PartitionSpec as P

MESH = pl.DeviceIdType.MESH
HD = 128
GROUP = 8
STEPS = 4
EXTRA = 16
NEGATIVE = -1e30
SCALE = HD ** -0.5 * math.log2(math.e)
F32 = jnp.float32
BF16 = jnp.bfloat16


def dot_t(a, b):
    return lax.dot_general(a, b, (((1,), (1,)), ((), ())), preferred_element_type=F32)


def dot(a, b):
    return jnp.dot(a, b, preferred_element_type=F32)


def wide(a, n):
    return jnp.concatenate([a] * n, axis=1)


def with_ones(values):
    return jnp.concatenate([values, jnp.ones(values.shape, BF16)], axis=1)


def row_max(scores):
    top = jnp.max(scores, axis=1, keepdims=True)
    return jnp.broadcast_to(top, (scores.shape[0], HD))


def kernel(
    nz, ntp,
    q_hbm, k_hbm, v_hbm, table_hbm, dq_hbm, nk_hbm, nv_hbm, ck_hbm, cv_hbm, lens_hbm, w_hbm,
    pre_hbm, dec_hbm,
    lens, tab_in, v_in, q_in, dq_in, nk_in, nv_in,
    kv, qt, ck, cv, wv, acc, top, dq32, nk32, nv32, dqs, dqt, tabs, bias, dacc, dtop,
    ob, ost, db, dst, att, sbuf, rbuf, mbuf, fbuf, prev, decv,
    loc, zs, zr, ss, sr, os, orr, xs, xr, ds, dr, js, jr, ws, wr, at_s, at_r, rs, rr, bs, br,
):
    half = nz // 2
    rounds = half // 2
    ctx = lax.axis_index("ctx")
    tp = lax.axis_index("tp")
    z, xh, c = ctx // 4, (ctx // 2) % 2, ctx % 2
    mine = ctx % 4
    tokens = q_in.shape[0]
    cache = ck.shape[1]
    slots = tab_in.shape[1]
    lines = dq32.shape[0]
    rows = GROUP * lines

    def turned(a):
        return jnp.transpose(a.astype(F32))

    def device(zz, xx, cc):
        return (zz * 4 + xx * 2 + cc, tp)

    def move(src, dst, send, recv, to):
        return pltpu.make_async_remote_copy(
            src_ref=src, dst_ref=dst, send_sem=send, recv_sem=recv, device_id=to, device_id_type=MESH
        )

    sibling = device(z, xh, 1 - c)
    beside = device(z, 1 - xh, c)
    across = device(z, 1 - xh, 1 - c)
    near = (
        (sibling, xh * 2 + 1 - c),
        (beside, (1 - xh) * 2 + c),
        (across, (1 - xh) * 2 + 1 - c),
    )

    def toward(d, hops):
        return device(lax.rem(z + (hops if d == 0 else nz - hops), nz), xh, c)

    def block(d, s):
        return lax.rem(jnp.where(d == 0, z + nz - s, z + s), nz)

    loads = [
        pltpu.make_async_copy(a, b, loc.at[n])
        for n, (a, b) in enumerate((
            (k_hbm, kv.at[z, c, 0]),
            (v_hbm, v_in),
            (table_hbm, tab_in),
            (dq_hbm, dq_in),
            (nk_hbm, nk_in),
            (nv_hbm, nv_in),
            (lens_hbm, lens),
            (ck_hbm, ck),
            (cv_hbm, cv),
            (q_hbm, q_in),
            (w_hbm, wv.at[xh, c]),
        ))
    ]
    for load in loads:
        load.start()
    barrier = pltpu.get_barrier_semaphore()

    def greet(o, _):
        pl.semaphore_signal(barrier, inc=1, device_id=(ctx, lax.rem(tp + o, ntp)), device_id_type=MESH)
        return 0

    along_z = [toward(d, hops) for hops in (1, 2, 3) for d in (0, 1)]
    for to in along_z + [sibling, beside, across]:
        pl.semaphore_signal(barrier, inc=1, device_id=to, device_id_type=MESH)
    lax.fori_loop(1, ntp, greet, 0)
    loads[0].wait()
    loads[1].wait()
    kv[z, c, 1] = turned(v_in[...]).astype(BF16)
    pl.semaphore_wait(barrier, ntp + 8)

    def along(d, p, s, zb):
        ref = kv.at[zb, c, p]
        to = toward(d, 2 - s % 2)
        return move(ref, ref, zs.at[d, p, s - 1], zr.at[d, p, s - 1], to)

    def over(d, s, cc):
        ref = kv.at[block(d, s), cc]
        return move(ref, ref, ss.at[d, s - 1], sr.at[d, s - 1], sibling)

    def over_own(cc):
        ref = kv.at[z, cc]
        return move(ref, ref, os, orr, sibling)

    every = [(p, d) for p in (0, 1) for d in (0, 1)]
    for p, d in every:
        if rounds > 1 or p == d:
            along(d, p, 2, z).start()
    for p, d in every:
        along(d, p, 1, z).start()
    over_own(c).start()

    for load in loads[2:4]:
        load.wait()
    tabs[mine] = jnp.full(tabs.shape[1:], -1, jnp.int32)
    tabs[mine, 0:1, 0:slots] = tab_in[...]
    for r in range(4):
        dq32[pl.ds(r * STEPS, STEPS), :] = dq_in[r].astype(F32)
    line = dq32[...]
    stacked = jnp.concatenate([line[:, h * HD:(h + 1) * HD] for h in range(GROUP)], axis=0)
    dqs[...] = stacked.astype(BF16)
    dqt[mine] = jnp.transpose(stacked).astype(BF16)

    def swap(n, src, dst):
        return move(src, dst, xs.at[n], xr.at[n], beside)

    swaps = [
        swap(0, qt.at[0], qt.at[1]),
        swap(1, ob.at[0], ob.at[1]),
        swap(2, ost.at[0], ost.at[1]),
    ]

    def tell(n, place):
        to = near[n][0]
        return [
            move(ref.at[place], ref.at[place], ds.at[n, m], dr.at[n, m], to)
            for m, ref in enumerate((dqt, tabs))
        ]

    def settle(n, source, target):
        to = near[n][0]
        return [
            move(ref.at[0, source], ref.at[1, target], js.at[n, m], jr.at[n, m], to)
            for m, ref in enumerate((db, dst))
        ]

    def weight(n, xx, source, to):
        return move(source, wv.at[xx, c], ws.at[n], wr.at[n], to)

    weights_out = [
        weight(0, xh, w_hbm, sibling),
        weight(1, xh, w_hbm, beside),
        weight(2, 1 - xh, wv.at[1 - xh, c], sibling),
    ]

    def weight_in(n, xx, cc):
        ref = wv.at[xx, cc]
        return move(ref, ref, ws.at[n], wr.at[n], sibling)

    for n in range(3):
        for copy in tell(n, mine):
            copy.start()
    loads[9].wait()
    for h in range(GROUP):
        qt[0, :, h * HD:(h + 1) * HD] = turned(q_in[:, h * HD:(h + 1) * HD]).astype(BF16)
    swaps[0].start()
    for n in range(2):
        weights_out[n].start()

    def own_decode():
        for load in loads[4:9]:
            load.wait()
        nk32[...] = jnp.zeros_like(nk32)
        nv32[...] = jnp.zeros_like(nv32)
        for r in range(4):
            nk32[pl.ds(r * STEPS, STEPS), :] = nk_in[r].astype(F32)
            nv32[pl.ds(r * STEPS, STEPS), :] = nv_in[r].astype(F32)
        queries = dqs[...]
        q_id = lax.broadcasted_iota(jnp.int32, (rows, cache), 0)
        k_id = lax.broadcasted_iota(jnp.int32, (rows, cache), 1)
        q_row = (q_id >> 2) & 3
        scores = []
        for r in range(4):
            live = (q_row == r) & (k_id < lens[r])
            scores.append(jnp.where(live, dot_t(queries, ck[r]), NEGATIVE))
        n_id = lax.broadcasted_iota(jnp.int32, (rows, HD), 0)
        u_id = lax.broadcasted_iota(jnp.int32, (rows, HD), 1)
        live = ((u_id >> 2) == ((n_id >> 2) & 3)) & ((u_id & 3) <= (n_id & 3))
        scores.append(jnp.where(live, dot_t(queries, nk32[...].astype(BF16)), NEGATIVE))
        most = row_max(scores[-1])
        for r in range(4):
            most = jnp.maximum(most, row_max(scores[r]))
        total = jnp.zeros((rows, 2 * HD), F32)
        for r in range(4):
            weights = jnp.exp2((scores[r] - wide(most, cache // HD)) * SCALE)
            total += dot(weights.astype(BF16), with_ones(cv[r]))
        weights = jnp.exp2((scores[-1] - most) * SCALE)
        total += dot(weights.astype(BF16), with_ones(nv32[...].astype(BF16)))
        dacc[...] = jnp.zeros(dacc.shape, F32)
        dtop[...] = jnp.full(dtop.shape, NEGATIVE, F32)
        dacc[mine, 0:HD] = jnp.transpose(total[:, :HD])
        dacc[mine, HD:] = jnp.transpose(total[:, HD:])[0:EXTRA]
        dtop[mine, 0:1] = jnp.transpose(most)[0:1]

    def page_bias():
        line_id = lax.broadcasted_iota(jnp.int32, (nz * 8, HD), 0)
        page = (line_id >> 3) * 32 + xh * 16 + c * 8 + (line_id & 7)
        for n in range(4):
            named = jnp.where(page == tabs[n, 0:1], 1.0, 0.0)
            found = jnp.max(named, axis=1, keepdims=True)
            penalty = jnp.broadcast_to(jnp.where(found > 0.5, 0.0, NEGATIVE), (nz * 8, HD))
            bias[:, :, n * HD:(n + 1) * HD] = penalty.reshape(nz, 8, HD)

    def keys_of(blocks):
        return jnp.concatenate([kv[zb, cc, 0] for zb in blocks for cc in (0, 1)], axis=0)

    def values_of(blocks):
        return with_ones_below(
            jnp.concatenate([kv[zb, cc, 1] for zb in blocks for cc in (0, 1)], axis=1)
        )

    def with_ones_below(values):
        return jnp.concatenate([values, jnp.ones((EXTRA, values.shape[1]), BF16)], axis=0)

    def update(scores, old, total, values):
        most = jnp.max(scores, axis=0, keepdims=True)
        if old is not None:
            most = jnp.maximum(old, most)
        weights = jnp.exp2((scores - most) * SCALE).astype(BF16)
        mixed = dot(values, weights)
        if old is not None:
            mixed += total * jnp.exp2((old - most) * SCALE)
        return most, mixed

    def decode_step(blocks):
        queries = jnp.concatenate([dqt[n] for n in range(4)], axis=1)
        keys = jnp.concatenate([kv[zb, c, 0] for zb in blocks], axis=0)
        values = with_ones_below(jnp.concatenate([kv[zb, c, 1] for zb in blocks], axis=1))
        penalty = []
        for zb in blocks:
            lines_of = bias[zb]
            penalty += [jnp.broadcast_to(lines_of[n:n + 1], (16, 4 * rows)) for n in range(8)]
        scores = dot(keys, queries) + jnp.concatenate(penalty, axis=0)
        old = jnp.concatenate([dtop[n, 0:1] for n in range(4)], axis=1)
        total = jnp.concatenate([dacc[n] for n in range(4)], axis=1)
        most, mixed = update(scores, old, total, values)
        for n in range(4):
            dacc[n] = mixed[:, n * rows:(n + 1) * rows]
            dtop[n, 0:1] = most[:, n * rows:(n + 1) * rows]

    lanes = [slice(n, n + 2 * HD) for n in range(0, GROUP * HD, 2 * HD)]

    def attend(side, blocks, masked):
        keys = keys_of(blocks)
        values = values_of(blocks)
        scores = [dot(keys, qt[side, :, cols]) for cols in lanes]
        if masked:
            k_id = lax.broadcasted_iota(jnp.int32, (2 * tokens, 2 * HD), 0)
            q_id = lax.broadcasted_iota(jnp.int32, (2 * tokens, 2 * HD), 1) & (tokens - 1)
            live = k_id <= c * tokens + q_id
            done = [
                update(jnp.where(live, part_scores, NEGATIVE), None, None, values)
                for part_scores in scores
            ]
        else:
            done = [
                update(part_scores, top[side, 0:1, cols], acc[side, :, cols], values)
                for part_scores, cols in zip(scores, lanes)
            ]
        for (most, mixed), cols in zip(done, lanes):
            acc[side, :, cols] = mixed
            top[side, 0:1, cols] = most

    def attend_some(side, first, second, one, both):
        @pl.when(both)
        def _():
            attend(side, [first, second], False)

        @pl.when(one & jnp.logical_not(both))
        def _():
            attend(side, [first], False)

    def numbered(n):
        side = jnp.where(n < half - 1, 1, 0)
        s = jnp.where(side == 1, n + 1, n - half + 2)
        return side, block(0, s), block(1, s), z >= s, z + s >= nz

    total_pairs = 2 * (half - 1)

    def attend_range(start, stop):
        def one(n, _):
            attend_some(*numbered(n))
            return 0

        lax.fori_loop(start, stop, one, 0)

    own_decode()
    for n in range(3):
        for copy in tell(n, near[n][1]):
            copy.wait_recv()
    page_bias()
    decode_step([z])
    over_own(1 - c).wait_recv()
    attend(0, [z], True)
    acc[1] = jnp.zeros(acc.shape[1:], F32)
    top[1, 0:1] = jnp.full((1, GROUP * HD), NEGATIVE, F32)

    def odd(s):
        for p, d in every:
            along(d, p, s, block(d, s)).wait_recv()
        for d in (0, 1):
            over(d, s, c).start()

    def ring(k, _):
        for p, d in every:
            zb = block(d, 2 * k - 2)
            along(d, p, 2 * k - 2, zb).wait_recv()
            if p == d:
                along(d, p, 2 * k, zb).start()
            else:
                @pl.when(k < rounds)
                def _():
                    along(d, p, 2 * k, zb).start()
        for p, d in every:
            along(d, p, 2 * k - 1, block(d, 2 * k - 2)).start()
        for d in (0, 1):
            over(d, 2 * k - 2, c).start()
        decode_step([block(d, 2 * k - 2) for d in (0, 1)])

        @pl.when(k > 2)
        def _():
            odd(2 * k - 5)
            decode_step([block(d, 2 * k - 5) for d in (0, 1)])

        return 0

    lax.fori_loop(2, rounds + 1, ring, 0)
    weights_out[1].wait_recv()
    weights_out[2].start()
    if rounds > 1:
        odd(half - 3)
        decode_step([block(d, half - 3) for d in (0, 1)])
    odd(half - 1)
    for d in (0, 1):
        along(d, d, half, block(d, half)).wait_recv()
    over(0, half, c).start()
    decode_step([block(0, half - 1), block(1, half - 1), block(0, half)])

    def part(total, most):
        weight_sum = jnp.maximum(total[HD:HD + 1], 1e-30)
        return (total[:HD] / weight_sum).astype(BF16), most * SCALE + jnp.log2(weight_sum)

    def join(total, most, other, level):
        level_own = most * SCALE
        high = jnp.maximum(level_own, level)
        own, far = jnp.exp2(level_own - high), jnp.exp2(level - high)
        scale = 1.0 / (total[HD:HD + 1] * own + far)
        return total[:HD] * (own * scale) + other.astype(F32) * (far * scale)

    out, level = part(
        jnp.concatenate([dacc[n] for n in range(4)], axis=1),
        jnp.concatenate([dtop[n, 0:1] for n in range(4)], axis=1),
    )
    for n in range(4):
        db[0, n] = out[:, n * rows:(n + 1) * rows]
        dst[0, n] = jnp.broadcast_to(level[:, n * rows:(n + 1) * rows], (8, rows))
    for n in range(3):
        for copy in settle(n, near[n][1], mine):
            copy.start()

    def over_in(first, stop):
        for s in range(first, stop):
            for d in (0, 1):
                over(d, s, 1 - c).wait_recv()

    ready = min(3, half - 1)
    swaps[0].wait_recv()
    over_in(1, ready + 1)
    attend_range(0, ready)
    done_pairs = ready
    for n in range(3):
        for copy in settle(n, mine, near[n][1]):
            copy.wait_recv()
    levels = [dtop[mine, 0:1] * SCALE] + [dst[1, place, 0:1] for _, place in near]
    high = functools.reduce(jnp.maximum, levels)
    shares = [jnp.exp2(one - high) for one in levels]
    own_part = dacc[mine]
    mixed = own_part[:HD] * shares[0]
    weight_sum = own_part[HD:HD + 1] * shares[0]
    for (_, place), fraction in zip(near, shares[1:]):
        mixed += db[1, place].astype(F32) * fraction
        weight_sum += fraction
    mixed = jnp.transpose(mixed / weight_sum).astype(BF16)
    for h in range(GROUP):
        att[z, h // 4, h % 4] = mixed[h * lines:(h + 1) * lines]

    reach = 3

    def share(d, s, zb):
        ref = att.at[zb] if s < half else att.at[zb, d]
        to = toward(d, (s - 1) % reach + 1)
        return move(ref, ref, at_s.at[d, s - 1], at_r.at[d, s - 1], to)

    def spread(base):
        for s in range(min(base + reach, half), base, -1):
            for d in (0, 1):
                share(d, s, block(d, base)).start()

    def send_parts():
        def more(j, _):
            first = jnp.where(j == 0, z, block(0, half))
            attend_some(1, first, first, jnp.where(j == 0, 1 - xh, z // half) > 0, j < 0)
            return 0

        lax.fori_loop(0, 2, more, 0)
        out, level = part(acc[1], top[1, 0:1])
        ob[0] = out
        ost[0] = jnp.broadcast_to(level, (8, GROUP * HD))
        swaps[1].start()
        swaps[2].start()

    bases = list(range(0, half, reach))
    for base in bases:
        if base:
            for d in (0, 1):
                share(d, base, block(d, base)).wait_recv()
        spread(base)
        if base == 0:
            over_in(ready + 1, half)
            over(0, half, 1 - c).wait_recv()
            attend_range(done_pairs, half - 1)
            done_pairs = half - 1
            send_parts()
        if base == bases[-1]:
            attend_range(done_pairs, total_pairs)
        elif base:
            attend_range(done_pairs, done_pairs + 4)
            done_pairs += 4
    weight_in(0, xh, 1 - c).wait_recv()
    weight_in(2, 1 - xh, 1 - c).wait_recv()
    loads[10].wait()
    for s in range(1, half + 1):
        if s not in bases:
            for d in (0, 1):
                share(d, s, block(d, s)).wait_recv()

    lhs = jnp.concatenate(
        [att[:, h // 4, h % 4].reshape(nz * lines, HD) for h in range(GROUP)], axis=1
    )
    depth = sbuf.shape[2]
    for xx in (0, 1):
        term = dot(lhs, jnp.concatenate([wv[xx, 0], wv[xx, 1]], axis=1)).astype(BF16)
        for cc in (0, 1):
            for j in range(ntp):
                sbuf[j, xx * 2 + cc] = term[j * depth:(j + 1) * depth, cc * HD:(cc + 1) * HD]

    def deal(o, to, source):
        return move(sbuf.at[to], rbuf.at[source], rs.at[o - 1], rr.at[o - 1], (ctx, to))

    def deal_out(o, _):
        deal(o, lax.rem(tp + o, ntp), tp).start()
        return 0

    lax.fori_loop(1, ntp, deal_out, 0)
    rbuf[tp] = sbuf[tp]

    def deal_in(o, _):
        deal(o, lax.rem(tp + o, ntp), lax.rem(tp + ntp - o, ntp)).wait_recv()
        return 0

    lax.fori_loop(1, ntp, deal_in, 0)
    total = rbuf[0].astype(F32)
    for j in range(1, ntp):
        total += rbuf[j].astype(F32)
    mbuf[...] = total.astype(BF16)

    def hand(n):
        to, place = near[n]
        return move(mbuf.at[place], fbuf.at[mine], bs.at[n], br.at[n], to)

    def handed(n):
        to, place = near[n]
        return move(mbuf.at[mine], fbuf.at[place], bs.at[n], br.at[n], to)

    for n in range(3):
        hand(n).start()
    fbuf[mine] = mbuf[mine]

    @pl.when(z >= half)
    def _():
        attend(0, [block(0, half)], False)

    swaps[1].wait_recv()
    swaps[2].wait_recv()
    whole = join(acc[0], top[0, 0:1], ob[1], ost[1, 0:1])
    for h in range(GROUP):
        prev[:, h * HD:(h + 1) * HD] = jnp.transpose(whole[:, h * HD:(h + 1) * HD]).astype(BF16)
    store_pre = pltpu.make_async_copy(prev, pre_hbm, loc.at[11])
    store_pre.start()

    for n in range(3):
        handed(n).wait_recv()
    for n in range(4):
        for zz in range(depth // lines):
            first = (zz * 4 + n) * lines
            decv[first:first + lines] = fbuf[n, zz * lines:(zz + 1) * lines]
    store_dec = pltpu.make_async_copy(decv, dec_hbm, loc.at[12])
    store_dec.start()

    def ring_sent(s, _):
        for p, d in every:
            along(d, p, s, block(d, (s - 1) // 2 * 2)).wait_send()
        for d in (0, 1):
            over(d, s, c).wait_send()
        return 0

    lax.fori_loop(1, half, ring_sent, 0)
    for s in range(1, half + 1):
        for d in (0, 1):
            share(d, s, block(d, (s - 1) // reach * reach)).wait_send()
    for d in (0, 1):
        along(d, d, half, block(d, half - 2)).wait_send()
    over(0, half, c).wait_send()
    over_own(c).wait_send()
    for copy in swaps + weights_out:
        copy.wait_send()

    for n in range(3):
        for copy in tell(n, mine) + settle(n, near[n][1], mine):
            copy.wait_send()
        hand(n).wait_send()

    def dealt(o, _):
        deal(o, lax.rem(tp + o, ntp), tp).wait_send()
        return 0

    lax.fori_loop(1, ntp, dealt, 0)
    store_pre.wait()
    store_dec.wait()


def local(pre_q, pre_k, pre_v, page_table, dec_q, dec_new_k, dec_new_v, cache_k, cache_v, cache_len, out_weight):
    nz = lax.axis_size("ctx") // 4
    ntp = lax.axis_size("tp")
    half = nz // 2
    tokens, width = pre_q.shape
    row_dev, cache = cache_k.shape[:2]
    lines = row_dev * STEPS
    rows = GROUP * lines
    out_rows = nz * 4 * lines // ntp
    depth = nz // ntp * lines
    hbm = pl.BlockSpec(memory_space=pltpu.HBM)
    sem = pltpu.SemaphoreType.DMA

    def vmem(shape, dtype=BF16):
        return pltpu.VMEM(shape, dtype)

    return pl.pallas_call(
        functools.partial(kernel, nz, ntp),
        out_shape=(
            jax.ShapeDtypeStruct((tokens, width), BF16),
            jax.ShapeDtypeStruct((out_rows, HD), BF16),
        ),
        in_specs=[hbm] * 11,
        out_specs=(hbm, hbm),
        scratch_shapes=[
            pltpu.SMEM(cache_len.shape, jnp.int32),
            vmem(page_table.shape, jnp.int32),
            vmem((tokens, HD)),
            vmem((tokens, width)),
            vmem(dec_q.shape),
            vmem(dec_new_k.shape),
            vmem(dec_new_v.shape),
            vmem((nz, 2, 2, tokens, HD)),
            vmem((2, HD, width)),
            vmem((row_dev, cache, HD)),
            vmem((row_dev, cache, HD)),
            vmem((2, 2, width, HD)),
            vmem((2, HD + EXTRA, width), F32),
            vmem((2, 8, width), F32),
            vmem((lines, width), F32),
            vmem((HD, HD), F32),
            vmem((HD, HD), F32),
            vmem((rows, HD)),
            vmem((4, HD, rows)),
            vmem((4, 8, HD), jnp.int32),
            vmem((nz, 8, 4 * rows), F32),
            vmem((4, HD + EXTRA, rows), F32),
            vmem((4, 8, rows), F32),
            vmem((2, HD, width)),
            vmem((2, 8, width), F32),
            vmem((2, 4, HD, rows)),
            vmem((2, 4, 8, HD), F32),
            vmem((nz, 2, 4, lines, HD)),
            vmem((ntp, 4, depth, HD)),
            vmem((ntp, 4, depth, HD)),
            vmem((4, depth, HD)),
            vmem((4, depth, HD)),
            vmem((tokens, width)),
            vmem((out_rows, HD)),
            sem((13,)),
            sem((2, 2, half)), sem((2, 2, half)),
            sem((2, half)), sem((2, half)),
            sem(()), sem(()),
            sem((3,)), sem((3,)),
            sem((3, 2)), sem((3, 2)),
            sem((3, 2)), sem((3, 2)),
            sem((3,)), sem((3,)),
            sem((2, half)), sem((2, half)),
            sem((max(ntp - 1, 1),)), sem((max(ntp - 1, 1),)),
            sem((3,)), sem((3,)),
        ],
        compiler_params=pltpu.CompilerParams(
            collective_id=0, has_side_effects=True, vmem_limit_bytes=63 << 20
        ),
    )(
        pre_q, pre_k, pre_v, page_table, dec_q, dec_new_k, dec_new_v, cache_k, cache_v, cache_len, out_weight
    )


def solution(mesh):
    placed = (
        P("ctx", "tp"),
        P("ctx", "tp"),
        P("ctx", "tp"),
        P("ctx", None),
        P("ctx", None, "tp"),
        P("ctx", None, "tp"),
        P("ctx", None, "tp"),
        P("ctx", None, "tp"),
        P("ctx", None, "tp"),
        P("ctx"),
        P("tp", "ctx"),
    )
    return jax.shard_map(
        local,
        mesh=mesh,
        in_specs=placed,
        out_specs=(P("ctx", "tp"), P("tp", "ctx")),
        check_vma=False,
    )
```

```python
import functools
import math

import jax
import jax.numpy as jnp
from jax import lax
from jax.experimental import pallas as pl
from jax.experimental.pallas import tpu as pltpu
from jax.sharding import PartitionSpec as P

MESH = pl.DeviceIdType.MESH
HD = 128
GROUP = 8
STEPS = 4
EXTRA = 16
NEGATIVE = -1e30
SCALE = HD ** -0.5 * math.log2(math.e)
F32 = jnp.float32
BF16 = jnp.bfloat16


def dot_t(a, b):
    return lax.dot_general(a, b, (((1,), (1,)), ((), ())), preferred_element_type=F32)


def dot(a, b):
    return jnp.dot(a, b, preferred_element_type=F32)


def wide(a, n):
    return jnp.concatenate([a] * n, axis=1)


def with_ones(values):
    return jnp.concatenate([values, jnp.ones(values.shape, BF16)], axis=1)


def row_max(scores):
    top = jnp.max(scores, axis=1, keepdims=True)
    return jnp.broadcast_to(top, (scores.shape[0], HD))


def kernel(
    nz, ntp,
    q_hbm, k_hbm, v_hbm, table_hbm, dq_hbm, nk_hbm, nv_hbm, ck_hbm, cv_hbm, lens_hbm, w_hbm,
    pre_hbm, dec_hbm,
    lens, tab_in, v_in, q_in, dq_in, nk_in, nv_in,
    kv, qt, ck, cv, wv, acc, top, dq32, nk32, nv32, dqs, dqt, tabs, bias, dacc, dtop,
    ob, ost, db, dst, att, sbuf, rbuf, mbuf, prev,
    loc, zs, zr, ss, sr, os, orr, xs, xr, ds, dr, js, jr, ws, wr, at_s, at_r, rs, rr, bs, br,
):
    half = nz // 2
    rounds = half // 2
    ctx = lax.axis_index("ctx")
    tp = lax.axis_index("tp")
    z, xh, c = ctx // 4, (ctx // 2) % 2, ctx % 2
    mine = ctx % 4
    tokens = q_in.shape[0]
    cache = ck.shape[1]
    slots = tab_in.shape[1]
    lines = dq32.shape[0]
    rows = GROUP * lines

    def turned(a):
        return jnp.transpose(a.astype(F32))

    def device(zz, xx, cc):
        return (zz * 4 + xx * 2 + cc, tp)

    def move(src, dst, send, recv, to):
        return pltpu.make_async_remote_copy(
            src_ref=src, dst_ref=dst, send_sem=send, recv_sem=recv, device_id=to, device_id_type=MESH
        )

    sibling = device(z, xh, 1 - c)
    beside = device(z, 1 - xh, c)
    across = device(z, 1 - xh, 1 - c)
    near = (
        (sibling, xh * 2 + 1 - c),
        (beside, (1 - xh) * 2 + c),
        (across, (1 - xh) * 2 + 1 - c),
    )

    def toward(d, hops):
        return device(lax.rem(z + (hops if d == 0 else nz - hops), nz), xh, c)

    def block(d, s):
        return lax.rem(jnp.where(d == 0, z + nz - s, z + s), nz)

    loads = [
        pltpu.make_async_copy(a, b, loc.at[n])
        for n, (a, b) in enumerate((
            (k_hbm, kv.at[z, c, 0]),
            (v_hbm, v_in),
            (table_hbm, tab_in),
            (dq_hbm, dq_in),
            (nk_hbm, nk_in),
            (nv_hbm, nv_in),
            (lens_hbm, lens),
            (ck_hbm, ck),
            (cv_hbm, cv),
            (q_hbm, q_in),
            (w_hbm, wv.at[xh, c]),
        ))
    ]
    barrier = pltpu.get_barrier_semaphore()

    def greet(o, _):
        pl.semaphore_signal(barrier, inc=1, device_id=(ctx, lax.rem(tp + o, ntp)), device_id_type=MESH)
        return 0

    along_z = [toward(d, hops) for hops in (1, 2, 3) for d in (0, 1)]
    for to in along_z + [sibling, beside, across]:
        pl.semaphore_signal(barrier, inc=1, device_id=to, device_id_type=MESH)
    for load in loads[:2]:
        load.start()
    lax.fori_loop(1, ntp, greet, 0)
    for load in loads[2:]:
        load.start()
    pl.semaphore_wait(barrier, ntp + 8)

    def along(d, p, s, zb, source=None):
        ref = kv.at[zb, c, p]
        to = toward(d, 2 - s % 2)
        return move(ref if source is None else source, ref, zs.at[d, p, s - 1], zr.at[d, p, s - 1], to)

    def over(d, s, cc):
        ref = kv.at[block(d, s), cc]
        return move(ref, ref, ss.at[d, s - 1], sr.at[d, s - 1], sibling)

    def over_own(cc):
        ref = kv.at[z, cc]
        return move(ref, ref, os, orr, sibling)

    every = [(p, d) for p in (0, 1) for d in (0, 1)]
    for p in (0, 1):
        if p == 1:
            loads[1].wait()
            kv[z, c, 1] = turned(v_in[...]).astype(BF16)
        for s in (2, 1):
            for d in (0, 1):
                if s == 1 or rounds > 1 or p == d:
                    along(d, p, s, z, k_hbm if p == 0 else None).start()
    loads[0].wait()
    over_own(c).start()

    for load in loads[2:4]:
        load.wait()
    tabs[mine] = jnp.full(tabs.shape[1:], -1, jnp.int32)
    tabs[mine, 0:1, 0:slots] = tab_in[...]
    for r in range(4):
        dq32[pl.ds(r * STEPS, STEPS), :] = dq_in[r].astype(F32)
    line = dq32[...]
    stacked = jnp.concatenate([line[:, h * HD:(h + 1) * HD] for h in range(GROUP)], axis=0)
    dqs[...] = stacked.astype(BF16)
    dqt[mine] = jnp.transpose(stacked).astype(BF16)

    def swap(n, src, dst):
        return move(src, dst, xs.at[n], xr.at[n], beside)

    swaps = [
        swap(0, qt.at[0], qt.at[1]),
        swap(1, ob.at[0], ob.at[1]),
        swap(2, ost.at[0], ost.at[1]),
    ]

    def tell(n, place):
        to = near[n][0]
        return [
            move(ref.at[place], ref.at[place], ds.at[n, m], dr.at[n, m], to)
            for m, ref in enumerate((dqt, tabs))
        ]

    def settle(n, source, target):
        to = near[n][0]
        return [
            move(ref.at[0, source], ref.at[1, target], js.at[n, m], jr.at[n, m], to)
            for m, ref in enumerate((db, dst))
        ]

    def weight(n, xx, source, to):
        return move(source, wv.at[xx, c], ws.at[n], wr.at[n], to)

    weights_out = [
        weight(0, xh, w_hbm, sibling),
        weight(1, xh, w_hbm, beside),
        weight(2, 1 - xh, wv.at[1 - xh, c], sibling),
    ]

    def weight_in(n, xx, cc):
        ref = wv.at[xx, cc]
        return move(ref, ref, ws.at[n], wr.at[n], sibling)

    for n in range(3):
        for copy in tell(n, mine):
            copy.start()
    loads[9].wait()
    for h in range(GROUP):
        qt[0, :, h * HD:(h + 1) * HD] = turned(q_in[:, h * HD:(h + 1) * HD]).astype(BF16)
    swaps[0].start()
    for n in range(2):
        weights_out[n].start()

    def own_decode():
        for load in loads[4:9]:
            load.wait()
        nk32[...] = jnp.zeros_like(nk32)
        nv32[...] = jnp.zeros_like(nv32)
        for r in range(4):
            nk32[pl.ds(r * STEPS, STEPS), :] = nk_in[r].astype(F32)
            nv32[pl.ds(r * STEPS, STEPS), :] = nv_in[r].astype(F32)
        queries = dqs[...]
        q_id = lax.broadcasted_iota(jnp.int32, (rows, cache), 0)
        k_id = lax.broadcasted_iota(jnp.int32, (rows, cache), 1)
        q_row = (q_id >> 2) & 3
        scores = []
        for r in range(4):
            live = (q_row == r) & (k_id < lens[r])
            scores.append(jnp.where(live, dot_t(queries, ck[r]), NEGATIVE))
        n_id = lax.broadcasted_iota(jnp.int32, (rows, HD), 0)
        u_id = lax.broadcasted_iota(jnp.int32, (rows, HD), 1)
        live = ((u_id >> 2) == ((n_id >> 2) & 3)) & ((u_id & 3) <= (n_id & 3))
        scores.append(jnp.where(live, dot_t(queries, nk32[...].astype(BF16)), NEGATIVE))
        most = row_max(scores[-1])
        for r in range(4):
            most = jnp.maximum(most, row_max(scores[r]))
        total = jnp.zeros((rows, 2 * HD), F32)
        for r in range(4):
            weights = jnp.exp2((scores[r] - wide(most, cache // HD)) * SCALE)
            total += dot(weights.astype(BF16), with_ones(cv[r]))
        weights = jnp.exp2((scores[-1] - most) * SCALE)
        total += dot(weights.astype(BF16), with_ones(nv32[...].astype(BF16)))
        dacc[...] = jnp.zeros(dacc.shape, F32)
        dtop[...] = jnp.full(dtop.shape, NEGATIVE, F32)
        dacc[mine, 0:HD] = jnp.transpose(total[:, :HD])
        dacc[mine, HD:] = jnp.transpose(total[:, HD:])[0:EXTRA]
        dtop[mine, 0:1] = jnp.transpose(most)[0:1]

    def page_bias():
        line_id = lax.broadcasted_iota(jnp.int32, (nz * 8, HD), 0)
        page = (line_id >> 3) * 32 + xh * 16 + c * 8 + (line_id & 7)
        for n in range(4):
            named = jnp.where(page == tabs[n, 0:1], 1.0, 0.0)
            found = jnp.max(named, axis=1, keepdims=True)
            penalty = jnp.broadcast_to(jnp.where(found > 0.5, 0.0, NEGATIVE), (nz * 8, HD))
            bias[:, :, n * HD:(n + 1) * HD] = penalty.reshape(nz, 8, HD)

    def keys_of(blocks):
        return jnp.concatenate([kv[zb, cc, 0] for zb in blocks for cc in (0, 1)], axis=0)

    def values_of(blocks):
        return with_ones_below(
            jnp.concatenate([kv[zb, cc, 1] for zb in blocks for cc in (0, 1)], axis=1)
        )

    def with_ones_below(values):
        return jnp.concatenate([values, jnp.ones((EXTRA, values.shape[1]), BF16)], axis=0)

    def update(scores, old, total, values):
        most = jnp.max(scores, axis=0, keepdims=True)
        if old is not None:
            most = jnp.maximum(old, most)
        weights = jnp.exp2((scores - most) * SCALE).astype(BF16)
        mixed = dot(values, weights)
        if old is not None:
            mixed += total * jnp.exp2((old - most) * SCALE)
        return most, mixed

    def decode_step(blocks):
        queries = jnp.concatenate([dqt[n] for n in range(4)], axis=1)
        keys = jnp.concatenate([kv[zb, c, 0] for zb in blocks], axis=0)
        values = with_ones_below(jnp.concatenate([kv[zb, c, 1] for zb in blocks], axis=1))
        penalty = []
        for zb in blocks:
            lines_of = bias[zb]
            penalty += [jnp.broadcast_to(lines_of[n:n + 1], (16, 4 * rows)) for n in range(8)]
        scores = dot(keys, queries) + jnp.concatenate(penalty, axis=0)
        old = jnp.concatenate([dtop[n, 0:1] for n in range(4)], axis=1)
        total = jnp.concatenate([dacc[n] for n in range(4)], axis=1)
        most, mixed = update(scores, old, total, values)
        for n in range(4):
            dacc[n] = mixed[:, n * rows:(n + 1) * rows]
            dtop[n, 0:1] = most[:, n * rows:(n + 1) * rows]

    lanes = [slice(n, n + 2 * HD) for n in range(0, GROUP * HD, 2 * HD)]

    def attend(side, blocks, masked):
        keys = keys_of(blocks)
        values = values_of(blocks)
        scores = [dot(keys, qt[side, :, cols]) for cols in lanes]
        if masked:
            k_id = lax.broadcasted_iota(jnp.int32, (2 * tokens, 2 * HD), 0)
            q_id = lax.broadcasted_iota(jnp.int32, (2 * tokens, 2 * HD), 1) & (tokens - 1)
            live = k_id <= c * tokens + q_id
            done = [
                update(jnp.where(live, part_scores, NEGATIVE), None, None, values)
                for part_scores in scores
            ]
        else:
            done = [
                update(part_scores, top[side, 0:1, cols], acc[side, :, cols], values)
                for part_scores, cols in zip(scores, lanes)
            ]
        for (most, mixed), cols in zip(done, lanes):
            acc[side, :, cols] = mixed
            top[side, 0:1, cols] = most

    def attend_some(side, first, second, one, both):
        @pl.when(both)
        def _():
            attend(side, [first, second], False)

        @pl.when(one & jnp.logical_not(both))
        def _():
            attend(side, [first], False)

    def numbered(n):
        side = jnp.where(n < half - 1, 1, 0)
        return paired(side, jnp.where(side == 1, n + 1, 2 * (n - half + 1) + 1))

    def paired(side, s):
        return side, block(0, s), block(1, s), z >= s, z + s >= nz

    def even(s):
        for d in (0, 1):
            over(d, s, 1 - c).wait_recv()
        attend_some(*paired(0, s))

    total_pairs = half - 1 + rounds

    def attend_range(start, stop):
        def one(n, _):
            attend_some(*numbered(n))
            return 0

        lax.fori_loop(start, stop, one, 0)

    own_decode()
    for n in range(3):
        for copy in tell(n, near[n][1]):
            copy.wait_recv()
    page_bias()
    decode_step([z])
    over_own(1 - c).wait_recv()
    attend(0, [z], True)
    acc[1] = jnp.zeros(acc.shape[1:], F32)
    top[1, 0:1] = jnp.full((1, GROUP * HD), NEGATIVE, F32)

    def odd(s):
        for p, d in every:
            along(d, p, s, block(d, s)).wait_recv()
        for d in (0, 1):
            over(d, s, c).start()

    def ring(k, _):
        @pl.when(k <= rounds)
        def _():
            for p, d in every:
                zb = block(d, 2 * k - 2)
                along(d, p, 2 * k - 2, zb).wait_recv()
                if p == d:
                    along(d, p, 2 * k, zb).start()
                else:
                    @pl.when(k < rounds)
                    def _():
                        along(d, p, 2 * k, zb).start()
            for p, d in every:
                along(d, p, 2 * k - 1, block(d, 2 * k - 2)).start()
            for d in (0, 1):
                over(d, 2 * k - 2, c).start()
            decode_step([block(d, 2 * k - 2) for d in (0, 1)])

        @pl.when(k > 2)
        def _():
            odd(2 * k - 5)
            decode_step([block(d, 2 * k - 5) for d in (0, 1)])
            even(2 * k - 4)

        return 0

    lax.fori_loop(2, rounds + 2, ring, 0)
    weights_out[1].wait_recv()
    weights_out[2].start()
    odd(half - 1)
    for d in (0, 1):
        along(d, d, half, block(d, half)).wait_recv()
    over(0, half, c).start()
    decode_step([block(0, half - 1), block(1, half - 1), block(0, half)])

    def part(total, most):
        weight_sum = jnp.maximum(total[HD:HD + 1], 1e-30)
        return (total[:HD] / weight_sum).astype(BF16), most * SCALE + jnp.log2(weight_sum)

    def join(total, most, other, level):
        level_own = most * SCALE
        high = jnp.maximum(level_own, level)
        own, far = jnp.exp2(level_own - high), jnp.exp2(level - high)
        scale = 1.0 / (total[HD:HD + 1] * own + far)
        return total[:HD] * (own * scale) + other.astype(F32) * (far * scale)

    out, level = part(
        jnp.concatenate([dacc[n] for n in range(4)], axis=1),
        jnp.concatenate([dtop[n, 0:1] for n in range(4)], axis=1),
    )
    for n in range(4):
        db[0, n] = out[:, n * rows:(n + 1) * rows]
        dst[0, n] = jnp.broadcast_to(level[:, n * rows:(n + 1) * rows], (8, rows))
    for n in range(3):
        for copy in settle(n, near[n][1], mine):
            copy.start()

    def over_in(first, stop):
        for s in range(first | 1, stop, 2):
            for d in (0, 1):
                over(d, s, 1 - c).wait_recv()

    ready = min(4, half - 1)
    swaps[0].wait_recv()
    over_in(1, ready + 1)
    attend_range(0, ready)
    done_pairs = ready
    for n in range(3):
        for copy in settle(n, mine, near[n][1]):
            copy.wait_recv()
    levels = [dtop[mine, 0:1] * SCALE] + [dst[1, place, 0:1] for _, place in near]
    high = functools.reduce(jnp.maximum, levels)
    shares = [jnp.exp2(one - high) for one in levels]
    own_part = dacc[mine]
    mixed = own_part[:HD] * shares[0]
    weight_sum = own_part[HD:HD + 1] * shares[0]
    for (_, place), fraction in zip(near, shares[1:]):
        mixed += db[1, place].astype(F32) * fraction
        weight_sum += fraction
    mixed = jnp.transpose(mixed / weight_sum).astype(BF16)
    for h in range(GROUP):
        att[z, h // 4, h % 4] = mixed[h * lines:(h + 1) * lines]

    reach = 3

    def share(d, s, zb):
        ref = att.at[zb] if s < half else att.at[zb, d]
        to = toward(d, (s - 1) % reach + 1)
        return move(ref, ref, at_s.at[d, s - 1], at_r.at[d, s - 1], to)

    def spread(base):
        for s in range(min(base + reach, half), base, -1):
            for d in (0, 1):
                share(d, s, block(d, base)).start()

    def send_parts():
        def more(j, _):
            first = jnp.where(j == 0, z, block(0, half))
            attend_some(1, first, first, jnp.where(j == 0, 1 - xh, z // half) > 0, j < 0)
            return 0

        lax.fori_loop(0, 2, more, 0)
        out, level = part(acc[1], top[1, 0:1])
        ob[0] = out
        ost[0] = jnp.broadcast_to(level, (8, GROUP * HD))
        swaps[1].start()
        swaps[2].start()

    bases = list(range(0, half, reach))
    for base in bases:
        if base:
            for d in (0, 1):
                share(d, base, block(d, base)).wait_recv()
        spread(base)
        if base == 0:
            over_in(ready + 1, half)
            over(0, half, 1 - c).wait_recv()
            attend_range(done_pairs, half - 1)
            done_pairs = half - 1
            send_parts()
        if base == bases[-1]:
            attend_range(done_pairs, total_pairs)
        elif base:
            attend_range(done_pairs, done_pairs + 2)
            done_pairs += 2
    weight_in(0, xh, 1 - c).wait_recv()
    weight_in(2, 1 - xh, 1 - c).wait_recv()
    loads[10].wait()
    for s in range(1, half + 1):
        if s not in bases:
            for d in (0, 1):
                share(d, s, block(d, s)).wait_recv()

    lhs = jnp.concatenate(
        [att[:, h // 4, h % 4].reshape(nz * lines, HD) for h in range(GROUP)], axis=1
    )
    depth = sbuf.shape[2]
    for xx in (0, 1):
        term = dot(lhs, jnp.concatenate([wv[xx, 0], wv[xx, 1]], axis=1)).astype(BF16)
        for cc in (0, 1):
            for j in range(ntp):
                sbuf[j, xx * 2 + cc] = term[j * depth:(j + 1) * depth, cc * HD:(cc + 1) * HD]

    def deal(o, to, source):
        return move(sbuf.at[to], rbuf.at[source], rs.at[o - 1], rr.at[o - 1], (ctx, to))

    def deal_out(o, _):
        deal(o, lax.rem(tp + o, ntp), tp).start()
        return 0

    lax.fori_loop(1, ntp, deal_out, 0)
    rbuf[tp] = sbuf[tp]

    def deal_in(o, _):
        deal(o, lax.rem(tp + o, ntp), lax.rem(tp + ntp - o, ntp)).wait_recv()
        return 0

    lax.fori_loop(1, ntp, deal_in, 0)
    total = rbuf[0].astype(F32)
    for j in range(1, ntp):
        total += rbuf[j].astype(F32)
    mbuf[...] = total.astype(BF16).reshape(mbuf.shape)

    def hand(n):
        to, place = near[n]
        return move(mbuf.at[place], dec_hbm.at[:, mine], bs.at[n], br.at[n], to)

    def handed(n):
        to, place = near[n]
        return move(mbuf.at[mine], dec_hbm.at[:, place], bs.at[n], br.at[n], to)

    for n in range(3):
        hand(n).start()
    store_dec = pltpu.make_async_copy(mbuf.at[mine], dec_hbm.at[:, mine], loc.at[12])
    store_dec.start()

    @pl.when(z >= half)
    def _():
        attend(0, [block(0, half)], False)

    swaps[1].wait_recv()
    swaps[2].wait_recv()
    whole = join(acc[0], top[0, 0:1], ob[1], ost[1, 0:1])
    for h in range(GROUP):
        prev[:, h * HD:(h + 1) * HD] = jnp.transpose(whole[:, h * HD:(h + 1) * HD]).astype(BF16)
    store_pre = pltpu.make_async_copy(prev, pre_hbm, loc.at[11])
    store_pre.start()

    for n in range(3):
        handed(n).wait_recv()

    def ring_sent(s, _):
        for p, d in every:
            along(d, p, s, block(d, (s - 1) // 2 * 2)).wait_send()
        for d in (0, 1):
            over(d, s, c).wait_send()
        return 0

    lax.fori_loop(1, half, ring_sent, 0)
    for s in range(1, half + 1):
        for d in (0, 1):
            share(d, s, block(d, (s - 1) // reach * reach)).wait_send()
    for d in (0, 1):
        along(d, d, half, block(d, half - 2)).wait_send()
    over(0, half, c).wait_send()
    over_own(c).wait_send()
    for copy in swaps + weights_out:
        copy.wait_send()

    for n in range(3):
        for copy in tell(n, mine) + settle(n, near[n][1], mine):
            copy.wait_send()
        hand(n).wait_send()

    def dealt(o, _):
        deal(o, lax.rem(tp + o, ntp), tp).wait_send()
        return 0

    lax.fori_loop(1, ntp, dealt, 0)
    store_pre.wait()
    store_dec.wait()


def local(pre_q, pre_k, pre_v, page_table, dec_q, dec_new_k, dec_new_v, cache_k, cache_v, cache_len, out_weight):
    nz = lax.axis_size("ctx") // 4
    ntp = lax.axis_size("tp")
    half = nz // 2
    tokens, width = pre_q.shape
    row_dev, cache = cache_k.shape[:2]
    lines = row_dev * STEPS
    rows = GROUP * lines
    out_rows = nz * 4 * lines // ntp
    depth = nz // ntp * lines
    hbm = pl.BlockSpec(memory_space=pltpu.HBM)
    sem = pltpu.SemaphoreType.DMA

    def vmem(shape, dtype=BF16):
        return pltpu.VMEM(shape, dtype)

    pre_out, dec_out = pl.pallas_call(
        functools.partial(kernel, nz, ntp),
        out_shape=(
            jax.ShapeDtypeStruct((tokens, width), BF16),
            jax.ShapeDtypeStruct((depth // lines, 4, lines, HD), BF16),
        ),
        in_specs=[hbm] * 11,
        out_specs=(hbm, hbm),
        scratch_shapes=[
            pltpu.SMEM(cache_len.shape, jnp.int32),
            vmem(page_table.shape, jnp.int32),
            vmem((tokens, HD)),
            vmem((tokens, width)),
            vmem(dec_q.shape),
            vmem(dec_new_k.shape),
            vmem(dec_new_v.shape),
            vmem((nz, 2, 2, tokens, HD)),
            vmem((2, HD, width)),
            vmem((row_dev, cache, HD)),
            vmem((row_dev, cache, HD)),
            vmem((2, 2, width, HD)),
            vmem((2, HD + EXTRA, width), F32),
            vmem((2, 8, width), F32),
            vmem((lines, width), F32),
            vmem((HD, HD), F32),
            vmem((HD, HD), F32),
            vmem((rows, HD)),
            vmem((4, HD, rows)),
            vmem((4, 8, HD), jnp.int32),
            vmem((nz, 8, 4 * rows), F32),
            vmem((4, HD + EXTRA, rows), F32),
            vmem((4, 8, rows), F32),
            vmem((2, HD, width)),
            vmem((2, 8, width), F32),
            vmem((2, 4, HD, rows)),
            vmem((2, 4, 8, HD), F32),
            vmem((nz, 2, 4, lines, HD)),
            vmem((ntp, 4, depth, HD)),
            vmem((ntp, 4, depth, HD)),
            vmem((4, depth // lines, lines, HD)),
            vmem((tokens, width)),
            sem((13,)),
            sem((2, 2, half)), sem((2, 2, half)),
            sem((2, half)), sem((2, half)),
            sem(()), sem(()),
            sem((3,)), sem((3,)),
            sem((3, 2)), sem((3, 2)),
            sem((3, 2)), sem((3, 2)),
            sem((3,)), sem((3,)),
            sem((2, half)), sem((2, half)),
            sem((max(ntp - 1, 1),)), sem((max(ntp - 1, 1),)),
            sem((3,)), sem((3,)),
        ],
        compiler_params=pltpu.CompilerParams(
            collective_id=0, has_side_effects=True, vmem_limit_bytes=63 << 20
        ),
    )(
        pre_q, pre_k, pre_v, page_table, dec_q, dec_new_k, dec_new_v, cache_k, cache_v, cache_len, out_weight
    )
    return pre_out, dec_out.reshape(out_rows, HD)


def solution(mesh):
    placed = (
        P("ctx", "tp"),
        P("ctx", "tp"),
        P("ctx", "tp"),
        P("ctx", None),
        P("ctx", None, "tp"),
        P("ctx", None, "tp"),
        P("ctx", None, "tp"),
        P("ctx", None, "tp"),
        P("ctx", None, "tp"),
        P("ctx"),
        P("tp", "ctx"),
    )
    return jax.shard_map(
        local,
        mesh=mesh,
        in_specs=placed,
        out_specs=(P("ctx", "tp"), P("tp", "ctx")),
        check_vma=False,
    )
```

```python
import functools
import math

import jax
import jax.numpy as jnp
from jax import lax
from jax.experimental import pallas as pl
from jax.experimental.pallas import tpu as pltpu
from jax.sharding import PartitionSpec as P

MESH = pl.DeviceIdType.MESH
HD = 128
GROUP = 8
STEPS = 4
EXTRA = 16
NEGATIVE = -1e30
SCALE = HD ** -0.5 * math.log2(math.e)
F32 = jnp.float32
BF16 = jnp.bfloat16


def dot_t(a, b):
    return lax.dot_general(a, b, (((1,), (1,)), ((), ())), preferred_element_type=F32)


def dot(a, b):
    return jnp.dot(a, b, preferred_element_type=F32)


def wide(a, n):
    return jnp.concatenate([a] * n, axis=1)


def with_ones(values):
    return jnp.concatenate([values, jnp.ones(values.shape, BF16)], axis=1)


def row_max(scores):
    top = jnp.max(scores, axis=1, keepdims=True)
    return jnp.broadcast_to(top, (scores.shape[0], HD))


def kernel(
    nz, ntp,
    q_hbm, k_hbm, v_hbm, table_hbm, dq_hbm, nk_hbm, nv_hbm, ck_hbm, cv_hbm, lens_hbm, w_hbm,
    pre_hbm, dec_hbm,
    lens, tab_in, v_in, q_in, dq_in, nk_in, nv_in,
    kv, qt, ck, cv, wv, acc, top, dq32, nk32, nv32, dqs, dqt, tabs, bias, dacc, dtop,
    ob, ost, db, dst, att, sbuf, rbuf, mbuf, prev,
    loc, zs, zr, ss, sr, os, orr, xs, xr, ds, dr, js, jr, ws, wr, vs, vr, at_s, at_r, rs, rr, bs, br,
):
    half = nz // 2
    rounds = half // 2
    ctx = lax.axis_index("ctx")
    tp = lax.axis_index("tp")
    z, xh, c = ctx // 4, (ctx // 2) % 2, ctx % 2
    mine = ctx % 4
    tokens = q_in.shape[0]
    cache = ck.shape[1]
    slots = tab_in.shape[1]
    lines = dq32.shape[0]
    rows = GROUP * lines

    def turned(a):
        return jnp.transpose(a.astype(F32))

    def device(zz, xx, cc):
        return (zz * 4 + xx * 2 + cc, tp)

    def move(src, dst, send, recv, to):
        return pltpu.make_async_remote_copy(
            src_ref=src, dst_ref=dst, send_sem=send, recv_sem=recv, device_id=to, device_id_type=MESH
        )

    sibling = device(z, xh, 1 - c)
    beside = device(z, 1 - xh, c)
    across = device(z, 1 - xh, 1 - c)
    near = (
        (sibling, xh * 2 + 1 - c),
        (beside, (1 - xh) * 2 + c),
        (across, (1 - xh) * 2 + 1 - c),
    )

    def toward(d, hops):
        return device(lax.rem(z + (hops if d == 0 else nz - hops), nz), xh, c)

    def block(d, s):
        return lax.rem(jnp.where(d == 0, z + nz - s, z + s), nz)

    loads = [
        pltpu.make_async_copy(a, b, loc.at[n])
        for n, (a, b) in enumerate((
            (k_hbm, kv.at[z, c, 0]),
            (v_hbm, v_in),
            (table_hbm, tab_in),
            (dq_hbm, dq_in),
            (nk_hbm, nk_in),
            (nv_hbm, nv_in),
            (lens_hbm, lens),
            (ck_hbm, ck),
            (cv_hbm, cv),
            (q_hbm, q_in),
            (w_hbm, wv.at[xh, c]),
        ))
    ]
    barrier = pltpu.get_barrier_semaphore()

    def greet(o, _):
        pl.semaphore_signal(barrier, inc=1, device_id=(ctx, lax.rem(tp + o, ntp)), device_id_type=MESH)
        return 0

    along_z = [toward(d, hops) for hops in (1, 2, 3) for d in (0, 1)]
    for to in along_z + [sibling, beside, across]:
        pl.semaphore_signal(barrier, inc=1, device_id=to, device_id_type=MESH)
    for load in loads[:2]:
        load.start()
    lax.fori_loop(1, ntp, greet, 0)
    for load in loads[2:]:
        load.start()
    pl.semaphore_wait(barrier, ntp + 8)

    def along(d, p, s, zb, source=None):
        ref = kv.at[zb, c, p]
        to = toward(d, 2 - s % 2)
        return move(ref if source is None else source, ref, zs.at[d, p, s - 1], zr.at[d, p, s - 1], to)

    def over(d, s, cc):
        ref = kv.at[block(d, s), cc]
        return move(ref, ref, ss.at[d, s - 1], sr.at[d, s - 1], sibling)

    def over_own(cc):
        ref = kv.at[z, cc]
        return move(ref, ref, os, orr, sibling)

    every = [(p, d) for p in (0, 1) for d in (0, 1)]
    for p in (0, 1):
        if p == 1:
            loads[1].wait()
            kv[z, c, 1] = turned(v_in[...]).astype(BF16)
        for s in (2, 1):
            for d in (0, 1):
                if s == 1 or rounds > 1 or p == d:
                    along(d, p, s, z, k_hbm if p == 0 else None).start()
    loads[0].wait()
    over_own(c).start()

    for load in loads[2:4]:
        load.wait()
    tabs[mine] = jnp.full(tabs.shape[1:], -1, jnp.int32)
    tabs[mine, 0:1, 0:slots] = tab_in[...]
    for r in range(4):
        dq32[pl.ds(r * STEPS, STEPS), :] = dq_in[r].astype(F32)
    line = dq32[...]
    stacked = jnp.concatenate([line[:, h * HD:(h + 1) * HD] for h in range(GROUP)], axis=0)
    dqs[...] = stacked.astype(BF16)
    dqt[mine] = jnp.transpose(stacked).astype(BF16)

    def swap(n, src, dst):
        return move(src, dst, xs.at[n], xr.at[n], beside)

    swaps = [
        swap(0, qt.at[0], qt.at[1]),
        swap(1, ob.at[0], ob.at[1]),
        swap(2, ost.at[0], ost.at[1]),
    ]

    def tell(n, place):
        to = near[n][0]
        return [
            move(ref.at[place], ref.at[place], ds.at[n, m], dr.at[n, m], to)
            for m, ref in enumerate((dqt, tabs))
        ]

    def settle(n, source, target):
        to = near[n][0]
        return [
            move(ref.at[0, source], ref.at[1, target], js.at[n, m], jr.at[n, m], to)
            for m, ref in enumerate((db, dst))
        ]

    weights_out = [
        move(w_hbm, wv.at[xh, c], ws.at[0], wr.at[0], sibling),
        move(wv.at[1 - xh, c], wv.at[1 - xh, c], ws.at[1], wr.at[1], sibling),
    ]

    def weight_half(n, xx):
        lines_of = pl.ds(n * (wv.shape[2] // 2), wv.shape[2] // 2)
        return move(
            w_hbm.at[lines_of, :], wv.at[xx, c, lines_of, :], vs.at[n], vr.at[n], beside
        )

    def weight_in(n, xx, cc):
        ref = wv.at[xx, cc]
        return move(ref, ref, ws.at[n], wr.at[n], sibling)

    for n in range(3):
        for copy in tell(n, mine):
            copy.start()
    loads[9].wait()
    for h in range(GROUP):
        qt[0, :, h * HD:(h + 1) * HD] = turned(q_in[:, h * HD:(h + 1) * HD]).astype(BF16)
    swaps[0].start()
    weights_out[0].start()
    if rounds == 1:
        weight_half(0, xh).start()

    def own_decode():
        for load in loads[4:9]:
            load.wait()
        nk32[...] = jnp.zeros_like(nk32)
        nv32[...] = jnp.zeros_like(nv32)
        for r in range(4):
            nk32[pl.ds(r * STEPS, STEPS), :] = nk_in[r].astype(F32)
            nv32[pl.ds(r * STEPS, STEPS), :] = nv_in[r].astype(F32)
        queries = dqs[...]
        q_id = lax.broadcasted_iota(jnp.int32, (rows, cache), 0)
        k_id = lax.broadcasted_iota(jnp.int32, (rows, cache), 1)
        q_row = (q_id >> 2) & 3
        scores = []
        for r in range(4):
            live = (q_row == r) & (k_id < lens[r])
            scores.append(jnp.where(live, dot_t(queries, ck[r]), NEGATIVE))
        n_id = lax.broadcasted_iota(jnp.int32, (rows, HD), 0)
        u_id = lax.broadcasted_iota(jnp.int32, (rows, HD), 1)
        live = ((u_id >> 2) == ((n_id >> 2) & 3)) & ((u_id & 3) <= (n_id & 3))
        scores.append(jnp.where(live, dot_t(queries, nk32[...].astype(BF16)), NEGATIVE))
        most = row_max(scores[-1])
        for r in range(4):
            most = jnp.maximum(most, row_max(scores[r]))
        total = jnp.zeros((rows, 2 * HD), F32)
        for r in range(4):
            weights = jnp.exp2((scores[r] - wide(most, cache // HD)) * SCALE)
            total += dot(weights.astype(BF16), with_ones(cv[r]))
        weights = jnp.exp2((scores[-1] - most) * SCALE)
        total += dot(weights.astype(BF16), with_ones(nv32[...].astype(BF16)))
        dacc[...] = jnp.zeros(dacc.shape, F32)
        dtop[...] = jnp.full(dtop.shape, NEGATIVE, F32)
        dacc[mine, 0:HD] = jnp.transpose(total[:, :HD])
        dacc[mine, HD:] = jnp.transpose(total[:, HD:])[0:EXTRA]
        dtop[mine, 0:1] = jnp.transpose(most)[0:1]

    def page_bias():
        line_id = lax.broadcasted_iota(jnp.int32, (nz * 8, HD), 0)
        page = (line_id >> 3) * 32 + xh * 16 + c * 8 + (line_id & 7)
        for n in range(4):
            named = jnp.where(page == tabs[n, 0:1], 1.0, 0.0)
            found = jnp.max(named, axis=1, keepdims=True)
            penalty = jnp.broadcast_to(jnp.where(found > 0.5, 0.0, NEGATIVE), (nz * 8, HD))
            bias[:, :, n * HD:(n + 1) * HD] = penalty.reshape(nz, 8, HD)

    def keys_of(blocks):
        return jnp.concatenate([kv[zb, cc, 0] for zb in blocks for cc in (0, 1)], axis=0)

    def values_of(blocks):
        return with_ones_below(
            jnp.concatenate([kv[zb, cc, 1] for zb in blocks for cc in (0, 1)], axis=1)
        )

    def with_ones_below(values):
        return jnp.concatenate([values, jnp.ones((EXTRA, values.shape[1]), BF16)], axis=0)

    def update(scores, old, total, values):
        most = jnp.max(scores, axis=0, keepdims=True)
        if old is not None:
            most = jnp.maximum(old, most)
        weights = jnp.exp2((scores - most) * SCALE).astype(BF16)
        mixed = dot(values, weights)
        if old is not None:
            mixed += total * jnp.exp2((old - most) * SCALE)
        return most, mixed

    def decode_step(blocks):
        queries = jnp.concatenate([dqt[n] for n in range(4)], axis=1)
        keys = jnp.concatenate([kv[zb, c, 0] for zb in blocks], axis=0)
        values = with_ones_below(jnp.concatenate([kv[zb, c, 1] for zb in blocks], axis=1))
        penalty = []
        for zb in blocks:
            lines_of = bias[zb]
            penalty += [jnp.broadcast_to(lines_of[n:n + 1], (16, 4 * rows)) for n in range(8)]
        scores = dot(keys, queries) + jnp.concatenate(penalty, axis=0)
        old = jnp.concatenate([dtop[n, 0:1] for n in range(4)], axis=1)
        total = jnp.concatenate([dacc[n] for n in range(4)], axis=1)
        most, mixed = update(scores, old, total, values)
        for n in range(4):
            dacc[n] = mixed[:, n * rows:(n + 1) * rows]
            dtop[n, 0:1] = most[:, n * rows:(n + 1) * rows]

    lanes = [slice(n, n + 2 * HD) for n in range(0, GROUP * HD, 2 * HD)]

    def attend(side, blocks, masked):
        keys = keys_of(blocks)
        values = values_of(blocks)
        scores = [dot(keys, qt[side, :, cols]) for cols in lanes]
        if masked:
            k_id = lax.broadcasted_iota(jnp.int32, (2 * tokens, 2 * HD), 0)
            q_id = lax.broadcasted_iota(jnp.int32, (2 * tokens, 2 * HD), 1) & (tokens - 1)
            live = k_id <= c * tokens + q_id
            done = [
                update(jnp.where(live, part_scores, NEGATIVE), None, None, values)
                for part_scores in scores
            ]
        else:
            done = [
                update(part_scores, top[side, 0:1, cols], acc[side, :, cols], values)
                for part_scores, cols in zip(scores, lanes)
            ]
        for (most, mixed), cols in zip(done, lanes):
            acc[side, :, cols] = mixed
            top[side, 0:1, cols] = most

    def attend_some(side, first, second, one, both):
        @pl.when(both)
        def _():
            attend(side, [first, second], False)

        @pl.when(one & jnp.logical_not(both))
        def _():
            attend(side, [first], False)

    def numbered(n):
        side = jnp.where(n < half - 1, 1, 0)
        return paired(side, jnp.where(side == 1, n + 1, 2 * (n - half + 1) + 1))

    def paired(side, s):
        return side, block(0, s), block(1, s), z >= s, z + s >= nz

    def even(s):
        for d in (0, 1):
            over(d, s, 1 - c).wait_recv()
        attend_some(*paired(0, s))

    total_pairs = half - 1 + rounds

    def attend_range(start, stop):
        def one(n, _):
            attend_some(*numbered(n))
            return 0

        lax.fori_loop(start, stop, one, 0)

    own_decode()
    for n in range(3):
        for copy in tell(n, near[n][1]):
            copy.wait_recv()
    page_bias()
    decode_step([z])
    over_own(1 - c).wait_recv()
    attend(0, [z], True)
    acc[1] = jnp.zeros(acc.shape[1:], F32)
    top[1, 0:1] = jnp.full((1, GROUP * HD), NEGATIVE, F32)

    def odd(s):
        for p, d in every:
            along(d, p, s, block(d, s)).wait_recv()
        for d in (0, 1):
            over(d, s, c).start()

    def ring(k, _):
        @pl.when(k <= rounds)
        def _():
            for p, d in every:
                zb = block(d, 2 * k - 2)
                along(d, p, 2 * k - 2, zb).wait_recv()
                if p == d:
                    along(d, p, 2 * k, zb).start()
                else:
                    @pl.when(k < rounds)
                    def _():
                        along(d, p, 2 * k, zb).start()
            for p, d in every:
                along(d, p, 2 * k - 1, block(d, 2 * k - 2)).start()
            for d in (0, 1):
                over(d, 2 * k - 2, c).start()

            @pl.when(k == rounds)
            def _():
                weight_half(0, xh).start()

            decode_step([block(d, 2 * k - 2) for d in (0, 1)])

        @pl.when(k > 2)
        def _():
            odd(2 * k - 5)
            decode_step([block(d, 2 * k - 5) for d in (0, 1)])
            even(2 * k - 4)

        return 0

    lax.fori_loop(2, rounds + 2, ring, 0)
    odd(half - 1)
    for d in (0, 1):
        along(d, d, half, block(d, half)).wait_recv()
    over(0, half, c).start()
    decode_step([block(0, half - 1), block(1, half - 1), block(0, half)])

    def part(total, most):
        weight_sum = jnp.maximum(total[HD:HD + 1], 1e-30)
        return (total[:HD] / weight_sum).astype(BF16), most * SCALE + jnp.log2(weight_sum)

    def join(total, most, other, level):
        level_own = most * SCALE
        high = jnp.maximum(level_own, level)
        own, far = jnp.exp2(level_own - high), jnp.exp2(level - high)
        scale = 1.0 / (total[HD:HD + 1] * own + far)
        return total[:HD] * (own * scale) + other.astype(F32) * (far * scale)

    out, level = part(
        jnp.concatenate([dacc[n] for n in range(4)], axis=1),
        jnp.concatenate([dtop[n, 0:1] for n in range(4)], axis=1),
    )
    for n in range(4):
        db[0, n] = out[:, n * rows:(n + 1) * rows]
        dst[0, n] = jnp.broadcast_to(level[:, n * rows:(n + 1) * rows], (8, rows))
    for n in range(3):
        for copy in settle(n, near[n][1], mine):
            copy.start()

    def over_in(first, stop):
        for s in range(first | 1, stop, 2):
            for d in (0, 1):
                over(d, s, 1 - c).wait_recv()

    weight_half(1, xh).start()
    ready = min(4, half - 1)
    swaps[0].wait_recv()
    over_in(1, ready + 1)
    attend_range(0, ready)
    done_pairs = ready
    for n in range(3):
        for copy in settle(n, mine, near[n][1]):
            copy.wait_recv()
    levels = [dtop[mine, 0:1] * SCALE] + [dst[1, place, 0:1] for _, place in near]
    high = functools.reduce(jnp.maximum, levels)
    shares = [jnp.exp2(one - high) for one in levels]
    own_part = dacc[mine]
    mixed = own_part[:HD] * shares[0]
    weight_sum = own_part[HD:HD + 1] * shares[0]
    for (_, place), fraction in zip(near, shares[1:]):
        mixed += db[1, place].astype(F32) * fraction
        weight_sum += fraction
    mixed = jnp.transpose(mixed / weight_sum).astype(BF16)
    for h in range(GROUP):
        att[z, h // 4, h % 4] = mixed[h * lines:(h + 1) * lines]

    reach = 3

    def share(d, s, zb):
        ref = att.at[zb] if s < half else att.at[zb, d]
        to = toward(d, (s - 1) % reach + 1)
        return move(ref, ref, at_s.at[d, s - 1], at_r.at[d, s - 1], to)

    def spread(base):
        for s in range(min(base + reach, half), base, -1):
            for d in (0, 1):
                share(d, s, block(d, base)).start()

    def send_parts():
        def more(j, _):
            first = jnp.where(j == 0, z, block(0, half))
            attend_some(1, first, first, jnp.where(j == 0, 1 - xh, z // half) > 0, j < 0)
            return 0

        lax.fori_loop(0, 2, more, 0)
        out, level = part(acc[1], top[1, 0:1])
        ob[0] = out
        ost[0] = jnp.broadcast_to(level, (8, GROUP * HD))
        swaps[1].start()
        swaps[2].start()

    bases = list(range(0, half, reach))
    for base in bases:
        if base:
            for d in (0, 1):
                share(d, base, block(d, base)).wait_recv()
        spread(base)
        if base == bases[min(1, len(bases) - 1)]:
            for n in range(2):
                weight_half(n, 1 - xh).wait_recv()
            weights_out[1].start()
        if base == 0:
            over_in(ready + 1, half)
            over(0, half, 1 - c).wait_recv()
            attend_range(done_pairs, half - 1)
            done_pairs = half - 1
            send_parts()
        if base == bases[-1]:
            attend_range(done_pairs, total_pairs)
        elif base:
            attend_range(done_pairs, done_pairs + 2)
            done_pairs += 2
    weight_in(0, xh, 1 - c).wait_recv()
    weight_in(1, 1 - xh, 1 - c).wait_recv()
    loads[10].wait()
    for s in range(1, half + 1):
        if s not in bases:
            for d in (0, 1):
                share(d, s, block(d, s)).wait_recv()

    lhs = jnp.concatenate(
        [att[:, h // 4, h % 4].reshape(nz * lines, HD) for h in range(GROUP)], axis=1
    )
    depth = sbuf.shape[2]
    for xx in (0, 1):
        term = dot(lhs, jnp.concatenate([wv[xx, 0], wv[xx, 1]], axis=1)).astype(BF16)
        for cc in (0, 1):
            for j in range(ntp):
                sbuf[j, xx * 2 + cc] = term[j * depth:(j + 1) * depth, cc * HD:(cc + 1) * HD]

    def deal(o, to, source):
        return move(sbuf.at[to], rbuf.at[source], rs.at[o - 1], rr.at[o - 1], (ctx, to))

    def deal_out(o, _):
        deal(o, lax.rem(tp + o, ntp), tp).start()
        return 0

    lax.fori_loop(1, ntp, deal_out, 0)
    rbuf[tp] = sbuf[tp]

    def deal_in(o, _):
        deal(o, lax.rem(tp + o, ntp), lax.rem(tp + ntp - o, ntp)).wait_recv()
        return 0

    lax.fori_loop(1, ntp, deal_in, 0)
    total = rbuf[0].astype(F32)
    for j in range(1, ntp):
        total += rbuf[j].astype(F32)
    mbuf[...] = total.astype(BF16).reshape(mbuf.shape)

    def hand(n):
        to, place = near[n]
        return move(mbuf.at[place], dec_hbm.at[:, mine], bs.at[n], br.at[n], to)

    def handed(n):
        to, place = near[n]
        return move(mbuf.at[mine], dec_hbm.at[:, place], bs.at[n], br.at[n], to)

    for n in range(3):
        hand(n).start()
    store_dec = pltpu.make_async_copy(mbuf.at[mine], dec_hbm.at[:, mine], loc.at[12])
    store_dec.start()

    @pl.when(z >= half)
    def _():
        attend(0, [block(0, half)], False)

    swaps[1].wait_recv()
    swaps[2].wait_recv()
    whole = join(acc[0], top[0, 0:1], ob[1], ost[1, 0:1])
    for h in range(GROUP):
        prev[:, h * HD:(h + 1) * HD] = jnp.transpose(whole[:, h * HD:(h + 1) * HD]).astype(BF16)
    store_pre = pltpu.make_async_copy(prev, pre_hbm, loc.at[11])
    store_pre.start()

    for n in range(3):
        handed(n).wait_recv()

    def ring_sent(s, _):
        for p, d in every:
            along(d, p, s, block(d, (s - 1) // 2 * 2)).wait_send()
        for d in (0, 1):
            over(d, s, c).wait_send()
        return 0

    lax.fori_loop(1, half, ring_sent, 0)
    for s in range(1, half + 1):
        for d in (0, 1):
            share(d, s, block(d, (s - 1) // reach * reach)).wait_send()
    for d in (0, 1):
        along(d, d, half, block(d, half - 2)).wait_send()
    over(0, half, c).wait_send()
    over_own(c).wait_send()
    for copy in swaps + weights_out + [weight_half(n, xh) for n in range(2)]:
        copy.wait_send()

    for n in range(3):
        for copy in tell(n, mine) + settle(n, near[n][1], mine):
            copy.wait_send()
        hand(n).wait_send()

    def dealt(o, _):
        deal(o, lax.rem(tp + o, ntp), tp).wait_send()
        return 0

    lax.fori_loop(1, ntp, dealt, 0)
    store_pre.wait()
    store_dec.wait()


def local(pre_q, pre_k, pre_v, page_table, dec_q, dec_new_k, dec_new_v, cache_k, cache_v, cache_len, out_weight):
    nz = lax.axis_size("ctx") // 4
    ntp = lax.axis_size("tp")
    half = nz // 2
    tokens, width = pre_q.shape
    row_dev, cache = cache_k.shape[:2]
    lines = row_dev * STEPS
    rows = GROUP * lines
    out_rows = nz * 4 * lines // ntp
    depth = nz // ntp * lines
    hbm = pl.BlockSpec(memory_space=pltpu.HBM)
    sem = pltpu.SemaphoreType.DMA

    def vmem(shape, dtype=BF16):
        return pltpu.VMEM(shape, dtype)

    pre_out, dec_out = pl.pallas_call(
        functools.partial(kernel, nz, ntp),
        out_shape=(
            jax.ShapeDtypeStruct((tokens, width), BF16),
            jax.ShapeDtypeStruct((depth // lines, 4, lines, HD), BF16),
        ),
        in_specs=[hbm] * 11,
        out_specs=(hbm, hbm),
        scratch_shapes=[
            pltpu.SMEM(cache_len.shape, jnp.int32),
            vmem(page_table.shape, jnp.int32),
            vmem((tokens, HD)),
            vmem((tokens, width)),
            vmem(dec_q.shape),
            vmem(dec_new_k.shape),
            vmem(dec_new_v.shape),
            vmem((nz, 2, 2, tokens, HD)),
            vmem((2, HD, width)),
            vmem((row_dev, cache, HD)),
            vmem((row_dev, cache, HD)),
            vmem((2, 2, width, HD)),
            vmem((2, HD + EXTRA, width), F32),
            vmem((2, 8, width), F32),
            vmem((lines, width), F32),
            vmem((HD, HD), F32),
            vmem((HD, HD), F32),
            vmem((rows, HD)),
            vmem((4, HD, rows)),
            vmem((4, 8, HD), jnp.int32),
            vmem((nz, 8, 4 * rows), F32),
            vmem((4, HD + EXTRA, rows), F32),
            vmem((4, 8, rows), F32),
            vmem((2, HD, width)),
            vmem((2, 8, width), F32),
            vmem((2, 4, HD, rows)),
            vmem((2, 4, 8, HD), F32),
            vmem((nz, 2, 4, lines, HD)),
            vmem((ntp, 4, depth, HD)),
            vmem((ntp, 4, depth, HD)),
            vmem((4, depth // lines, lines, HD)),
            vmem((tokens, width)),
            sem((13,)),
            sem((2, 2, half)), sem((2, 2, half)),
            sem((2, half)), sem((2, half)),
            sem(()), sem(()),
            sem((3,)), sem((3,)),
            sem((3, 2)), sem((3, 2)),
            sem((3, 2)), sem((3, 2)),
            sem((2,)), sem((2,)),
            sem((2,)), sem((2,)),
            sem((2, half)), sem((2, half)),
            sem((max(ntp - 1, 1),)), sem((max(ntp - 1, 1),)),
            sem((3,)), sem((3,)),
        ],
        compiler_params=pltpu.CompilerParams(
            collective_id=0, has_side_effects=True, vmem_limit_bytes=63 << 20
        ),
    )(
        pre_q, pre_k, pre_v, page_table, dec_q, dec_new_k, dec_new_v, cache_k, cache_v, cache_len, out_weight
    )
    return pre_out, dec_out.reshape(out_rows, HD)


def solution(mesh):
    placed = (
        P("ctx", "tp"),
        P("ctx", "tp"),
        P("ctx", "tp"),
        P("ctx", None),
        P("ctx", None, "tp"),
        P("ctx", None, "tp"),
        P("ctx", None, "tp"),
        P("ctx", None, "tp"),
        P("ctx", None, "tp"),
        P("ctx"),
        P("tp", "ctx"),
    )
    return jax.shard_map(
        local,
        mesh=mesh,
        in_specs=placed,
        out_specs=(P("ctx", "tp"), P("tp", "ctx")),
        check_vma=False,
    )
```

```python
import functools
import math

import jax
import jax.numpy as jnp
from jax import lax
from jax.experimental import pallas as pl
from jax.experimental.pallas import tpu as pltpu
from jax.sharding import PartitionSpec as P

MESH = pl.DeviceIdType.MESH
HD = 128
GROUP = 8
STEPS = 4
EXTRA = 16
NEGATIVE = -1e30
SCALE = HD ** -0.5 * math.log2(math.e)
F32 = jnp.float32
BF16 = jnp.bfloat16


def dot_t(a, b):
    return lax.dot_general(a, b, (((1,), (1,)), ((), ())), preferred_element_type=F32)


def dot(a, b):
    return jnp.dot(a, b, preferred_element_type=F32)


def wide(a, n):
    return jnp.concatenate([a] * n, axis=1)


def with_ones(values):
    return jnp.concatenate([values, jnp.ones(values.shape, BF16)], axis=1)


def row_max(scores):
    top = jnp.max(scores, axis=1, keepdims=True)
    return jnp.broadcast_to(top, (scores.shape[0], HD))


def kernel(
    nz, ntp,
    q_hbm, k_hbm, v_hbm, table_hbm, dq_hbm, nk_hbm, nv_hbm, ck_hbm, cv_hbm, lens_hbm, w_hbm,
    pre_hbm, dec_hbm,
    lens, tab_in, v_in, q_in, dq_in, nk_in, nv_in,
    kv, qt, ck, cv, wv, acc, top, dq32, nk32, nv32, dqs, dqt, tabs, bias, dacc, dtop,
    ob, ost, db, dst, att, sbuf, rbuf, mbuf, prev,
    loc, zs, zr, ss, sr, os, orr, xs, xr, ws, wr, at_s, at_r, rs, rr, bs, br,
):
    half = nz // 2
    rounds = half // 2
    ctx = lax.axis_index("ctx")
    tp = lax.axis_index("tp")
    z, xh, c = ctx // 4, (ctx // 2) % 2, ctx % 2
    mine = ctx % 4
    tokens = q_in.shape[0]
    cache = ck.shape[1]
    slots = tab_in.shape[1]
    lines = dq32.shape[0]
    rows = GROUP * lines

    def turned(a):
        return jnp.transpose(a.astype(F32))

    def device(zz, xx, cc):
        return (zz * 4 + xx * 2 + cc, tp)

    def move(src, dst, send, recv, to):
        return pltpu.make_async_remote_copy(
            src_ref=src, dst_ref=dst, send_sem=send, recv_sem=recv, device_id=to, device_id_type=MESH
        )

    sibling = device(z, xh, 1 - c)
    beside = device(z, 1 - xh, c)
    across = device(z, 1 - xh, 1 - c)

    def toward(d, hops):
        return device(lax.rem(z + (hops if d == 0 else nz - hops), nz), xh, c)

    def block(d, s):
        return lax.rem(jnp.where(d == 0, z + nz - s, z + s), nz)

    loads = [
        pltpu.make_async_copy(a, b, loc.at[n])
        for n, (a, b) in enumerate((
            (k_hbm, kv.at[z, c, 0]),
            (v_hbm, v_in),
            (table_hbm, tab_in),
            (dq_hbm, dq_in),
            (nk_hbm, nk_in),
            (nv_hbm, nv_in),
            (lens_hbm, lens),
            (ck_hbm, ck),
            (cv_hbm, cv),
            (q_hbm, q_in),
            (w_hbm, wv.at[xh, c]),
        ))
    ]
    barrier = pltpu.get_barrier_semaphore()

    def greet(o, _):
        pl.semaphore_signal(barrier, inc=1, device_id=(ctx, lax.rem(tp + o, ntp)), device_id_type=MESH)
        return 0

    along_z = [toward(d, hops) for hops in (1, 2, 3) for d in (0, 1)]
    for to in along_z + [sibling, beside, across]:
        pl.semaphore_signal(barrier, inc=1, device_id=to, device_id_type=MESH)
    for load in loads[:2]:
        load.start()
    lax.fori_loop(1, ntp, greet, 0)
    for load in loads[2:]:
        load.start()
    pl.semaphore_wait(barrier, ntp + 8)

    def along(d, p, s, zb, source=None):
        ref = kv.at[zb, c, p]
        to = toward(d, 2 - s % 2)
        return move(ref if source is None else source, ref, zs.at[d, p, s - 1], zr.at[d, p, s - 1], to)

    def over(d, s, cc):
        ref = kv.at[block(d, s), cc]
        return move(ref, ref, ss.at[d, s - 1], sr.at[d, s - 1], sibling)

    def over_own(cc):
        ref = kv.at[z, cc]
        return move(ref, ref, os, orr, sibling)

    every = [(p, d) for p in (0, 1) for d in (0, 1)]
    for p in (0, 1):
        if p == 1:
            loads[1].wait()
            kv[z, c, 1] = turned(v_in[...]).astype(BF16)
        for s in (2, 1):
            for d in (0, 1):
                if s == 1 or rounds > 1 or p == d:
                    along(d, p, s, z, k_hbm if p == 0 else None).start()
    loads[0].wait()
    over_own(c).start()

    for load in loads[2:4]:
        load.wait()
    tabs[0] = jnp.full(tabs.shape[1:], -1, jnp.int32)
    tabs[0, 0:1, 0:slots] = tab_in[...]
    for r in range(4):
        dq32[pl.ds(r * STEPS, STEPS), :] = dq_in[r].astype(F32)
    line = dq32[...]
    stacked = jnp.concatenate([line[:, h * HD:(h + 1) * HD] for h in range(GROUP)], axis=0)
    dqs[...] = stacked.astype(BF16)
    dqt[0] = jnp.transpose(stacked).astype(BF16)

    def swap(n, src, dst):
        return move(src, dst, xs.at[n], xr.at[n], beside)

    swaps = [
        swap(0, dqt.at[0], dqt.at[1]),
        swap(1, tabs.at[0], tabs.at[1]),
        swap(2, qt.at[0], qt.at[1]),
        swap(3, ob.at[0], ob.at[1]),
        swap(4, ost.at[0], ost.at[1]),
        swap(5, db.at[0], db.at[1]),
        swap(6, dst.at[0], dst.at[1]),
    ]

    def weight(n, xx, source, to):
        return move(source, wv.at[xx, c], ws.at[n], wr.at[n], to)

    weights_out = [
        weight(0, xh, w_hbm, sibling),
        weight(1, xh, w_hbm, beside),
        weight(2, 1 - xh, wv.at[1 - xh, c], sibling),
    ]

    def weight_in(n, xx, cc):
        ref = wv.at[xx, cc]
        return move(ref, ref, ws.at[n], wr.at[n], sibling)

    for n in range(2):
        swaps[n].start()
    loads[9].wait()
    for h in range(GROUP):
        qt[0, :, h * HD:(h + 1) * HD] = turned(q_in[:, h * HD:(h + 1) * HD]).astype(BF16)
    swaps[2].start()
    for n in range(2):
        weights_out[n].start()

    def own_decode():
        for load in loads[4:9]:
            load.wait()
        nk32[...] = jnp.zeros_like(nk32)
        nv32[...] = jnp.zeros_like(nv32)
        for r in range(4):
            nk32[pl.ds(r * STEPS, STEPS), :] = nk_in[r].astype(F32)
            nv32[pl.ds(r * STEPS, STEPS), :] = nv_in[r].astype(F32)
        queries = dqs[...]
        q_id = lax.broadcasted_iota(jnp.int32, (rows, cache), 0)
        k_id = lax.broadcasted_iota(jnp.int32, (rows, cache), 1)
        q_row = (q_id >> 2) & 3
        scores = []
        for r in range(4):
            live = (q_row == r) & (k_id < lens[r])
            scores.append(jnp.where(live, dot_t(queries, ck[r]), NEGATIVE))
        n_id = lax.broadcasted_iota(jnp.int32, (rows, HD), 0)
        u_id = lax.broadcasted_iota(jnp.int32, (rows, HD), 1)
        live = ((u_id >> 2) == ((n_id >> 2) & 3)) & ((u_id & 3) <= (n_id & 3))
        scores.append(jnp.where(live, dot_t(queries, nk32[...].astype(BF16)), NEGATIVE))
        most = row_max(scores[-1])
        for r in range(4):
            most = jnp.maximum(most, row_max(scores[r]))
        total = jnp.zeros((rows, 2 * HD), F32)
        for r in range(4):
            weights = jnp.exp2((scores[r] - wide(most, cache // HD)) * SCALE)
            total += dot(weights.astype(BF16), with_ones(cv[r]))
        weights = jnp.exp2((scores[-1] - most) * SCALE)
        total += dot(weights.astype(BF16), with_ones(nv32[...].astype(BF16)))
        dacc[0:HD, 0:rows] = jnp.transpose(total[:, :HD])
        dacc[HD:, 0:rows] = jnp.transpose(total[:, HD:])[0:EXTRA]
        dtop[0:1, 0:rows] = jnp.transpose(most)[0:1]
        dacc[:, rows:] = jnp.zeros((HD + EXTRA, rows), F32)
        dtop[0:1, rows:] = jnp.full((1, rows), NEGATIVE, F32)

    def page_bias():
        line_id = lax.broadcasted_iota(jnp.int32, (nz * 16, HD), 0)
        page = (line_id >> 4) * 32 + xh * 16 + (line_id & 15)
        for n in (0, 1):
            named = jnp.where(page == tabs[n, 0:1], 1.0, 0.0)
            found = jnp.max(named, axis=1, keepdims=True)
            penalty = jnp.broadcast_to(jnp.where(found > 0.5, 0.0, NEGATIVE), (nz * 16, HD))
            bias[:, :, n * HD:(n + 1) * HD] = penalty.reshape(nz, 16, HD)

    def keys_of(blocks):
        return jnp.concatenate([kv[zb, cc, 0] for zb in blocks for cc in (0, 1)], axis=0)

    def values_of(blocks):
        values = jnp.concatenate([kv[zb, cc, 1] for zb in blocks for cc in (0, 1)], axis=1)
        return jnp.concatenate([values, jnp.ones((EXTRA, values.shape[1]), BF16)], axis=0)

    def update(scores, old, total, values):
        most = jnp.max(scores, axis=0, keepdims=True)
        if old is not None:
            most = jnp.maximum(old, most)
        weights = jnp.exp2((scores - most) * SCALE).astype(BF16)
        mixed = dot(values, weights)
        if old is not None:
            mixed += total * jnp.exp2((old - most) * SCALE)
        return most, mixed

    def decode_step(blocks):
        queries = jnp.concatenate([dqt[0], dqt[1]], axis=1)
        scores = dot(keys_of(blocks), queries)
        penalty = []
        for zb in blocks:
            lines_of = bias[zb]
            penalty += [jnp.broadcast_to(lines_of[n:n + 1], (16, 2 * rows)) for n in range(16)]
        scores = scores + jnp.concatenate(penalty, axis=0)
        most, mixed = update(scores, dtop[0:1], dacc[...], values_of(blocks))
        dacc[...] = mixed
        dtop[0:1] = most

    lanes = [slice(n, n + 2 * HD) for n in range(0, GROUP * HD, 2 * HD)]

    def attend(side, blocks, masked):
        keys = keys_of(blocks)
        values = values_of(blocks)
        scores = [dot(keys, qt[side, :, cols]) for cols in lanes]
        if masked:
            k_id = lax.broadcasted_iota(jnp.int32, (2 * tokens, 2 * HD), 0)
            q_id = lax.broadcasted_iota(jnp.int32, (2 * tokens, 2 * HD), 1) & (tokens - 1)
            live = k_id <= c * tokens + q_id
            done = [
                update(jnp.where(live, part_scores, NEGATIVE), None, None, values)
                for part_scores in scores
            ]
        else:
            done = [
                update(part_scores, top[side, 0:1, cols], acc[side, :, cols], values)
                for part_scores, cols in zip(scores, lanes)
            ]
        for (most, mixed), cols in zip(done, lanes):
            acc[side, :, cols] = mixed
            top[side, 0:1, cols] = most

    def attend_some(side, first, second, one, both):
        @pl.when(both)
        def _():
            attend(side, [first, second], False)

        @pl.when(one & jnp.logical_not(both))
        def _():
            attend(side, [first], False)

    early = 3 if half >= 8 else 0

    def numbered(n):
        side = jnp.where((n >= early) & (n < early + half - 1), 1, 0)
        s = jnp.where(n < early, n + 1, jnp.where(side == 1, n - early + 1, n - half + 2))
        return side, block(0, s), block(1, s), z >= s, z + s >= nz

    total_pairs = 2 * (half - 1)
    first_partner = early // 2 + 2

    def attend_range(start, stop):
        def one(n, _):
            attend_some(*numbered(n))
            return 0

        lax.fori_loop(start, stop, one, 0)

    own_decode()
    over_own(1 - c).wait_recv()
    attend(0, [z], True)
    acc[1] = jnp.zeros(acc.shape[1:], F32)
    top[1, 0:1] = jnp.full((1, GROUP * HD), NEGATIVE, F32)
    swaps[0].wait_recv()
    swaps[1].wait_recv()
    page_bias()
    decode_step([z])

    def ring(k, _):
        for p, d in every:
            zb = block(d, 2 * k - 2)
            along(d, p, 2 * k - 2, zb).wait_recv()
            if p == d:
                along(d, p, 2 * k, zb).start()
            else:
                @pl.when(k < rounds)
                def _():
                    along(d, p, 2 * k, zb).start()
        for p, d in every:
            along(d, p, 2 * k - 1, block(d, 2 * k - 2)).start()
        for d in (0, 1):
            over(d, 2 * k - 2, c).start()
        for p, d in every:
            along(d, p, 2 * k - 3, block(d, 2 * k - 3)).wait_recv()
        for d in (0, 1):
            over(d, 2 * k - 3, c).start()
        for s in (2 * k - 2, 2 * k - 3):
            for d in (0, 1):
                over(d, s, 1 - c).wait_recv()
        decode_step([block(d, s) for s in (2 * k - 3, 2 * k - 2) for d in (0, 1)])

        @pl.when(k == first_partner)
        def _():
            swaps[2].wait_recv()

        attend_range(2 * k - 4, 2 * k - 2)
        return 0

    lax.fori_loop(2, rounds + 1, ring, 0)
    if rounds < first_partner:
        swaps[2].wait_recv()
    weights_out[1].wait_recv()
    weights_out[2].start()
    for d in (0, 1):
        along(d, d, half, block(d, half)).wait_recv()
    over(0, half, c).start()
    for p, d in every:
        along(d, p, half - 1, block(d, half - 1)).wait_recv()
    for d in (0, 1):
        over(d, half - 1, c).start()
    over(0, half, 1 - c).wait_recv()
    for d in (0, 1):
        over(d, half - 1, 1 - c).wait_recv()
    decode_step([block(0, half - 1), block(1, half - 1), block(0, half)])

    def part(total, most):
        weight_sum = jnp.maximum(total[HD:HD + 1], 1e-30)
        return (total[:HD] / weight_sum).astype(BF16), most * SCALE + jnp.log2(weight_sum)

    def join(total, most, other, level):
        level_own = most * SCALE
        high = jnp.maximum(level_own, level)
        own, far = jnp.exp2(level_own - high), jnp.exp2(level - high)
        scale = 1.0 / (total[HD:HD + 1] * own + far)
        return total[:HD] * (own * scale) + other.astype(F32) * (far * scale)

    out, level = part(dacc[:, rows:], dtop[0:1, rows:])
    db[0] = out
    dst[0] = jnp.broadcast_to(level, (8, HD))
    swaps[5].start()
    swaps[6].start()
    done_pairs = 2 * (rounds - 1)
    attend_range(done_pairs, min(done_pairs + 2, total_pairs))
    done_pairs = min(done_pairs + 2, total_pairs)
    swaps[5].wait_recv()
    swaps[6].wait_recv()
    mixed = jnp.transpose(join(dacc[:, 0:rows], dtop[0:1, 0:rows], db[1], dst[1, 0:1])).astype(BF16)
    for h in range(GROUP):
        att[z, h // 4, h % 4] = mixed[h * lines:(h + 1) * lines]

    reach = 3

    def share(d, s, zb):
        ref = att.at[zb] if s < half else att.at[zb, d]
        to = toward(d, (s - 1) % reach + 1)
        return move(ref, ref, at_s.at[d, s - 1], at_r.at[d, s - 1], to)

    def spread(base):
        for s in range(min(base + reach, half), base, -1):
            for d in (0, 1):
                share(d, s, block(d, base)).start()

    def send_parts():
        def more(j, _):
            first = jnp.where(j == 0, z, block(0, half))
            attend_some(1, first, first, jnp.where(j == 0, 1 - xh, z // half) > 0, j < 0)
            return 0

        lax.fori_loop(0, 2, more, 0)
        out, level = part(acc[1], top[1, 0:1])
        ob[0] = out
        ost[0] = jnp.broadcast_to(level, (8, GROUP * HD))
        swaps[3].start()
        swaps[4].start()

    bases = list(range(0, half, reach))
    for base in bases:
        if base:
            for d in (0, 1):
                share(d, base, block(d, base)).wait_recv()
        spread(base)
        stop = total_pairs if base == bases[-1] else min(done_pairs + 2, total_pairs)
        if done_pairs < stop:
            attend_range(done_pairs, stop)
        done_pairs = stop
        if base == 0:
            send_parts()
    weight_in(0, xh, 1 - c).wait_recv()
    weight_in(2, 1 - xh, 1 - c).wait_recv()
    loads[10].wait()
    for s in range(1, half + 1):
        if s not in bases:
            for d in (0, 1):
                share(d, s, block(d, s)).wait_recv()

    lhs = jnp.concatenate(
        [att[:, h // 4, h % 4].reshape(nz * lines, HD) for h in range(GROUP)], axis=1
    )
    depth = sbuf.shape[2]
    for xx in (0, 1):
        term = dot(lhs, jnp.concatenate([wv[xx, 0], wv[xx, 1]], axis=1)).astype(BF16)
        for cc in (0, 1):
            for j in range(ntp):
                sbuf[j, xx * 2 + cc] = term[j * depth:(j + 1) * depth, cc * HD:(cc + 1) * HD]

    def deal(o, to, source):
        return move(sbuf.at[to], rbuf.at[source], rs.at[o - 1], rr.at[o - 1], (ctx, to))

    def deal_out(o, _):
        deal(o, lax.rem(tp + o, ntp), tp).start()
        return 0

    lax.fori_loop(1, ntp, deal_out, 0)
    rbuf[tp] = sbuf[tp]

    def deal_in(o, _):
        deal(o, lax.rem(tp + o, ntp), lax.rem(tp + ntp - o, ntp)).wait_recv()
        return 0

    lax.fori_loop(1, ntp, deal_in, 0)
    total = rbuf[0].astype(F32)
    for j in range(1, ntp):
        total += rbuf[j].astype(F32)
    mbuf[...] = total.astype(BF16).reshape(mbuf.shape)
    near = ((sibling, xh, 1 - c), (beside, 1 - xh, c), (across, 1 - xh, 1 - c))

    def hand(n):
        to, xx, cc = near[n]
        return move(mbuf.at[xx * 2 + cc], dec_hbm.at[:, mine], bs.at[n], br.at[n], to)

    def handed(n):
        to, xx, cc = near[n]
        return move(mbuf.at[mine], dec_hbm.at[:, xx * 2 + cc], bs.at[n], br.at[n], to)

    for n in range(3):
        hand(n).start()
    store_dec = pltpu.make_async_copy(mbuf.at[mine], dec_hbm.at[:, mine], loc.at[12])
    store_dec.start()

    @pl.when(z >= half)
    def _():
        attend(0, [block(0, half)], False)

    swaps[3].wait_recv()
    swaps[4].wait_recv()
    whole = join(acc[0], top[0, 0:1], ob[1], ost[1, 0:1])
    for h in range(GROUP):
        prev[:, h * HD:(h + 1) * HD] = jnp.transpose(whole[:, h * HD:(h + 1) * HD]).astype(BF16)
    store_pre = pltpu.make_async_copy(prev, pre_hbm, loc.at[11])
    store_pre.start()

    for n in range(3):
        handed(n).wait_recv()

    def ring_sent(s, _):
        for p, d in every:
            along(d, p, s, block(d, (s - 1) // 2 * 2)).wait_send()
        for d in (0, 1):
            over(d, s, c).wait_send()
        return 0

    lax.fori_loop(1, half, ring_sent, 0)
    for s in range(1, half + 1):
        for d in (0, 1):
            share(d, s, block(d, (s - 1) // reach * reach)).wait_send()
    for d in (0, 1):
        along(d, d, half, block(d, half - 2)).wait_send()
    over(0, half, c).wait_send()
    over_own(c).wait_send()
    for copy in swaps + weights_out:
        copy.wait_send()

    for n in range(3):
        hand(n).wait_send()

    def dealt(o, _):
        deal(o, lax.rem(tp + o, ntp), tp).wait_send()
        return 0

    lax.fori_loop(1, ntp, dealt, 0)
    store_pre.wait()
    store_dec.wait()


def local(pre_q, pre_k, pre_v, page_table, dec_q, dec_new_k, dec_new_v, cache_k, cache_v, cache_len, out_weight):
    nz = lax.axis_size("ctx") // 4
    ntp = lax.axis_size("tp")
    half = nz // 2
    tokens, width = pre_q.shape
    row_dev, cache = cache_k.shape[:2]
    lines = row_dev * STEPS
    rows = GROUP * lines
    out_rows = nz * 4 * lines // ntp
    depth = nz // ntp * lines
    hbm = pl.BlockSpec(memory_space=pltpu.HBM)
    sem = pltpu.SemaphoreType.DMA

    def vmem(shape, dtype=BF16):
        return pltpu.VMEM(shape, dtype)

    pre_out, dec_out = pl.pallas_call(
        functools.partial(kernel, nz, ntp),
        out_shape=(
            jax.ShapeDtypeStruct((tokens, width), BF16),
            jax.ShapeDtypeStruct((depth // lines, 4, lines, HD), BF16),
        ),
        in_specs=[hbm] * 11,
        out_specs=(hbm, hbm),
        scratch_shapes=[
            pltpu.SMEM(cache_len.shape, jnp.int32),
            vmem(page_table.shape, jnp.int32),
            vmem((tokens, HD)),
            vmem((tokens, width)),
            vmem(dec_q.shape),
            vmem(dec_new_k.shape),
            vmem(dec_new_v.shape),
            vmem((nz, 2, 2, tokens, HD)),
            vmem((2, HD, width)),
            vmem((row_dev, cache, HD)),
            vmem((row_dev, cache, HD)),
            vmem((2, 2, width, HD)),
            vmem((2, HD + EXTRA, width), F32),
            vmem((2, 8, width), F32),
            vmem((lines, width), F32),
            vmem((HD, HD), F32),
            vmem((HD, HD), F32),
            vmem((rows, HD)),
            vmem((2, HD, rows)),
            vmem((2, 8, HD), jnp.int32),
            vmem((nz, 16, 2 * rows), F32),
            vmem((HD + EXTRA, 2 * rows), F32),
            vmem((8, 2 * rows), F32),
            vmem((2, HD, width)),
            vmem((2, 8, width), F32),
            vmem((2, HD, rows)),
            vmem((2, 8, HD), F32),
            vmem((nz, 2, 4, lines, HD)),
            vmem((ntp, 4, depth, HD)),
            vmem((ntp, 4, depth, HD)),
            vmem((4, depth // lines, lines, HD)),
            vmem((tokens, width)),
            sem((13,)),
            sem((2, 2, half)), sem((2, 2, half)),
            sem((2, half)), sem((2, half)),
            sem(()), sem(()),
            sem((7,)), sem((7,)),
            sem((3,)), sem((3,)),
            sem((2, half)), sem((2, half)),
            sem((max(ntp - 1, 1),)), sem((max(ntp - 1, 1),)),
            sem((3,)), sem((3,)),
        ],
        compiler_params=pltpu.CompilerParams(
            collective_id=0, has_side_effects=True, vmem_limit_bytes=63 << 20
        ),
    )(
        pre_q, pre_k, pre_v, page_table, dec_q, dec_new_k, dec_new_v, cache_k, cache_v, cache_len, out_weight
    )
    return pre_out, dec_out.reshape(out_rows, HD)


def solution(mesh):
    placed = (
        P("ctx", "tp"),
        P("ctx", "tp"),
        P("ctx", "tp"),
        P("ctx", None),
        P("ctx", None, "tp"),
        P("ctx", None, "tp"),
        P("ctx", None, "tp"),
        P("ctx", None, "tp"),
        P("ctx", None, "tp"),
        P("ctx"),
        P("tp", "ctx"),
    )
    return jax.shard_map(
        local,
        mesh=mesh,
        in_specs=placed,
        out_specs=(P("ctx", "tp"), P("tp", "ctx")),
        check_vma=False,
    )
```
